32 devices in a mesh: grp: 4 (over y, x), row: 8 (over z, core).
Axes of the slice: x: 2, y: 2, z: 4, core: 2. Of those that a mesh axis runs over, the one named last changes fastest.
Arguments:
- vectors: bfloat16 [131072, 1024], P(('grp', 'row')), may hold values from -6 to 6
- keep_bits: int32 [131072], P(('grp', 'row')), may hold values 0 or 1
- counts: int32 [1024], P(('grp', 'row')), may hold values from 1 to 128
- block_list: int32 [1024], replicated, may hold values from 0 to 2047, as said below
- home_pos: int32 [2048], replicated, may hold values from 0 to 2047, as said below
- old_centroids: bfloat16 [2048, 1024], P('grp'), may hold values from -1.5 to 1.5
Outputs:
- new_centroids: bfloat16 [2048, 1024], P(('grp', 'row'))
- scores: float32 [131072, 512], P(('grp', 'row'))
The draws below stay inside these ranges and needn't reach their ends.
Inputs may be any that keep to these rules, and one draw needn't show every extreme that they name: `block_list`: every block's list is one of the lists of the block's own group; on one device at most one block has a list whose new position lies in any given other group, and this most is reached in every draw. `home_pos`: A permutation of the positions; position p lies in group p // 512.
All inputs are finite; a program needn't handle non-finite values. No bound on the sum of `keep_bits` on one device may be relied on, other than what follows from the above.
Results may differ from the reference program's by a relative error of at most 0.002.
Values may be sent and summed in bfloat16 or wider, within the bound.
No kernel may reach another device: no remote copies, remote signals or barrier semaphores. Data moves between devices by JAX's collectives and lax.ppermute only.
A program may use at most 128 MiB of HBM per device.

```python
import math
import jax
import jax.numpy as jnp
from jax import lax

D = 1024
LISTS_GRP = 512
BLOCK = 128
PRIOR = 16
BLK_DEV = 32
BLOCKS = 1024
ROWS = 131072
LISTS = 2048
N_GRP = 4
N_ROW = 8


def draw_plan(key):
    base = jax.random.fold_in(key, 17)
    moved_per = LISTS_GRP // (2 * N_GRP)
    order_keys = jax.random.split(jax.random.fold_in(base, 1), N_GRP)
    orders = jax.vmap(lambda item: jax.random.permutation(item, LISTS_GRP))(order_keys).astype(jnp.int32)
    inverse = jnp.argsort(orders, axis=1, stable=True).astype(jnp.int32)
    group_ids = jnp.arange(N_GRP, dtype=jnp.int32)[:, None]
    slot_ids = jnp.arange(LISTS_GRP, dtype=jnp.int32)[None, :]
    leaves = orders < (N_GRP - 1) * moved_per
    direction = orders // moved_per
    within = orders % moved_per
    target = (group_ids + 1 + direction) % N_GRP
    back_dir = (group_ids - target - 1) % N_GRP
    wanted = jnp.clip(back_dir * moved_per + within, 0, LISTS_GRP - 1)
    target_safe = jnp.where(leaves, target, group_ids)
    new_slot = inverse[target_safe, wanted]
    homes = jnp.where(leaves, target * LISTS_GRP + new_slot, group_ids * LISTS_GRP + slot_ids)
    home_table = homes.reshape(-1).astype(jnp.int32)
    block_keys = jax.random.split(jax.random.fold_in(base, 2), N_GRP * N_ROW)
    perms = jax.vmap(lambda item: jax.random.permutation(item, BLK_DEV))(block_keys).astype(jnp.int32)
    place = jnp.argsort(perms, axis=1, stable=True).astype(jnp.int32).reshape(N_GRP, N_ROW, BLK_DEV)
    flags = jax.random.randint(jax.random.fold_in(base, 3), (N_GRP, N_ROW, BLK_DEV), 0, 2)
    forced_row = jax.random.randint(jax.random.fold_in(base, 4), (), 0, N_ROW)
    row_ids = jnp.arange(N_ROW, dtype=jnp.int32)[None, :, None]
    flags = jnp.where(row_ids == forced_row, 1, flags)
    moving = (place < N_GRP - 1) & (flags == 1)
    pick_move = jax.random.randint(jax.random.fold_in(base, 5), (N_GRP, N_ROW, BLK_DEV), 0, moved_per)
    stay_count = LISTS_GRP - (N_GRP - 1) * moved_per
    pick_stay = jax.random.randint(jax.random.fold_in(base, 6), (N_GRP, N_ROW, BLK_DEV), 0, stay_count)
    rank_wanted = jnp.where(moving, place * moved_per + pick_move, (N_GRP - 1) * moved_per + pick_stay)
    group_full = jnp.broadcast_to(jnp.arange(N_GRP, dtype=jnp.int32)[:, None, None], rank_wanted.shape)
    slots = inverse[group_full, rank_wanted]
    block_table = (group_full * LISTS_GRP + slots).reshape(-1).astype(jnp.int32)
    return (block_table, home_table)


def draw_block_list(key, part):
    return draw_plan(key)[0]


def draw_home_pos(key, part):
    return draw_plan(key)[1]


def with_ends(drawn, key, low, top_value):
    spot = [jax.random.randint(jax.random.fold_in(key, axis), (), 0, length) for axis, length in enumerate(drawn.shape)]
    longest = drawn.shape.index(max(drawn.shape))
    beside = spot[:longest] + [(spot[longest] + 1) % drawn.shape[longest]] + spot[longest + 1:]
    return drawn.at[tuple(spot)].set(low).at[tuple(beside)].set(top_value)


def levels(rng, shape, shards, low, high):
    factor_of, own = 1.0, jax.random.fold_in(rng, 6)
    for dim, shards_of in shards:
        steps = jnp.exp(jax.random.uniform(jax.random.fold_in(own, dim), (shards_of,), jnp.float32, low / len(shards), high / len(shards)))
        factor_of = factor_of * jnp.repeat(steps, shape[dim] // shards_of).reshape([-1 if axis == dim else 1 for axis in range(len(shape))])
    return factor_of


def noise(key, shape, width, limit, pieces=(), held_as=jnp.bfloat16):
    loudness = levels(key, shape, pieces, -0.22, 0.18) if pieces else 1.0
    entries = jax.random.normal(key, shape, jnp.float32) * width * loudness
    return jnp.minimum(jnp.maximum(entries, -limit), limit).astype(held_as)


def setup_inputs(seed: int = 0) -> dict:
    streams_of = jax.random.split(jax.random.key(seed), 7)
    vectors = noise(streams_of[0], (ROWS, D), 1.0, 6.0, ((0, 32),))
    keep_bits = with_ends((jax.random.randint(streams_of[1], (ROWS,), 0, 2) < 1).astype(jnp.int32), jax.random.fold_in(streams_of[1], 1), 0, 1)
    counts = with_ends(jax.random.randint(streams_of[2], (BLOCKS,), 1, BLOCK + 1), jax.random.fold_in(streams_of[2], 1), 1, BLOCK).astype(jnp.int32)
    block_list = draw_block_list(jax.random.fold_in(streams_of[6], 71), 0)
    home_pos = draw_home_pos(jax.random.fold_in(streams_of[6], 71), 0)
    old_centroids = noise(streams_of[5], (LISTS, D), 0.25, 1.5, ((0, 4),))
    return dict(vectors=vectors, keep_bits=keep_bits, counts=counts, block_list=block_list, home_pos=home_pos, old_centroids=old_centroids)


def centroid_rows(sums, totals, previous):
    prior_weight = 1.0 * PRIOR
    return ((sums + prior_weight * previous.astype(jnp.float32)) / (totals + prior_weight)[:, None]).astype(jnp.bfloat16)

def reference(vectors, keep_bits, counts, block_list, home_pos, old_centroids):
    blocks = counts.shape[0]
    row_blocks = vectors.reshape(blocks, BLOCK, D)
    position = jnp.arange(BLOCK, dtype=jnp.int32)[None, :]
    alive = (keep_bits.reshape(blocks, BLOCK) * (position < counts[:, None]).astype(jnp.int32)).astype(jnp.float32)

    def block_sum(item):
        rows, weights = item
        return jnp.dot(weights.astype(jnp.bfloat16), rows, preferred_element_type=jnp.float32)
    block_sums = lax.map(block_sum, (row_blocks, alive))
    block_counts = lax.optimization_barrier(jnp.sum(alive, axis=1))
    homes = jnp.take(home_pos, block_list).astype(jnp.int32)
    sums = jax.ops.segment_sum(block_sums, homes, num_segments=LISTS)
    totals = jax.ops.segment_sum(block_counts, homes, num_segments=LISTS)
    table = centroid_rows(sums, totals, old_centroids)
    norms = lax.optimization_barrier(jnp.sum(jnp.square(table.astype(jnp.float32)), axis=1))
    home_groups = (homes // LISTS_GRP).astype(jnp.int32)
    factor = 1.0 / math.sqrt(D)

    def block_scores(item):
        rows, weights, group_of = item
        start = (group_of * LISTS_GRP).astype(jnp.int32)
        part = lax.dynamic_slice_in_dim(table, start, LISTS_GRP, 0)
        part_norms = lax.dynamic_slice_in_dim(norms, start, LISTS_GRP, 0)
        dots = lax.dot_general(rows, part, (((1,), (1,)), ((), ())), preferred_element_type=jnp.float32)
        return (2.0 * dots - part_norms[None, :]) * factor * weights[:, None]
    scores = lax.map(block_scores, (row_blocks, alive, home_groups))
    return (table, scores.reshape(blocks * BLOCK, LISTS_GRP))
```

```python
import functools
import math

import jax
import jax.numpy as jnp
from jax import lax
from jax.experimental import pallas as pl
from jax.experimental.pallas import tpu as pltpu
from jax.sharding import PartitionSpec as P

PRIOR = 16
MIB = 1 << 20
F32 = jnp.float32
BF16 = jnp.bfloat16
ROW_DIMS = (((1,), (1,)), ((), ()))
COL_DIMS = (((0,), (0,)), ((), ()))
VMEM = pl.BlockSpec(memory_space=pltpu.VMEM)
SMEM = pl.BlockSpec(memory_space=pltpu.SMEM)
HBM = pl.BlockSpec(memory_space=pl.ANY)


def peer(index, step, size):
    if size & (size - 1) == 0:
        return index ^ step
    return (index + step) % size


def power(exponent):
    return jnp.exp2(exponent).astype(BF16).astype(F32)


def iota(shape, dim):
    return lax.broadcasted_iota(jnp.int32, shape, dim)


def movers_kernel(
    n_groups, lists_group, list_ref, pos_ref, counts_ref, keep_ref, vec_ref, alive_ref, meta_ref, picks_ref, *rest
):
    steps = n_groups - 1
    head_refs, row_refs, (held, sems) = rest[:steps], rest[steps : 2 * steps], rest[2 * steps :]
    blocks, block = keep_ref.shape
    group = lax.axis_index("grp")
    base = (group * lax.axis_size("row") + lax.axis_index("row")) * blocks
    lane = iota((1, block), 1)
    row = iota((blocks, block), 0)
    slots = jnp.full((1, block), -1, jnp.int32)
    filled = jnp.zeros((blocks, block), jnp.int32)
    picks = [jnp.int32(-1)] * steps
    homes = [jnp.int32(-1)] * steps
    for b in range(blocks):
        home = pos_ref[list_ref[base + b]]
        home_group = home // lists_group
        slot = home - home_group * lists_group
        slots = jnp.where((lane == b) & (home_group == group), slot, slots)
        filled = jnp.where(row == b, counts_ref[b], filled)
        for k in range(steps):
            hit = home_group == peer(group, k + 1, n_groups)
            picks[k] = jnp.where(hit, b, picks[k])
            homes[k] = jnp.where(hit, slot, homes[k])
    fetches = []
    for k in range(steps):
        picks_ref[k] = picks[k]
        start = pl.multiple_of(jnp.maximum(picks[k], 0) * block, block)
        fetches.append(pltpu.make_async_copy(vec_ref.at[pl.ds(start, block), :], held.at[k], sems.at[k]))
        fetches[k].start()
    alive = keep_ref[...].astype(F32) * (iota((blocks, block), 1) < filled).astype(F32)
    alive_ref[...] = alive
    ones = jnp.ones((8, block), BF16)
    block_counts = lax.dot_general(ones, alive.astype(BF16), ROW_DIMS, preferred_element_type=F32)
    meta_ref[...] = jnp.zeros_like(meta_ref)
    meta_ref[0:1, :] = slots.astype(F32)
    meta_ref[1:2, 0:blocks] = block_counts[0:1, :]
    stores = []
    for k in range(steps):
        fetches[k].wait()
        stores.append(pltpu.make_async_copy(held.at[k], row_refs[k], sems.at[steps + k]))
        stores[k].start()
        weights = alive_ref[pl.ds(jnp.maximum(picks[k], 0), 1), :]
        wide = jnp.broadcast_to(weights, (16, block)).astype(BF16)
        total = jnp.dot(wide, held[k], preferred_element_type=F32)
        for j in range(total.shape[1] // 128):
            head_refs[k][j : j + 1, :] = total[0:1, j * 128 : (j + 1) * 128]
        tail = total.shape[1] // 128
        head_refs[k][tail : tail + 8, :] = jnp.concatenate(
            [
                jnp.broadcast_to(jnp.sum(weights, axis=1, keepdims=True), (1, 128)),
                jnp.broadcast_to(homes[k].astype(F32), (1, 128)),
                jnp.zeros((6, 128), F32),
            ],
            axis=0,
        )
    for k in range(steps):
        stores[k].wait()


def movers(n_groups, lists_group, block_list, home_pos, counts, keep, vectors):
    steps = n_groups - 1
    blocks, block = keep.shape
    width = vectors.shape[1]
    outs = pl.pallas_call(
        functools.partial(movers_kernel, n_groups, lists_group),
        out_shape=[
            jax.ShapeDtypeStruct((blocks, block), F32),
            jax.ShapeDtypeStruct((8, block), F32),
            jax.ShapeDtypeStruct((steps,), jnp.int32),
        ]
        + [jax.ShapeDtypeStruct((width // 128 + 8, 128), F32)] * steps
        + [jax.ShapeDtypeStruct((block, width), BF16)] * steps,
        in_specs=[SMEM, SMEM, SMEM, VMEM, HBM],
        out_specs=[VMEM, VMEM, SMEM] + [VMEM] * steps + [HBM] * steps,
        scratch_shapes=[pltpu.VMEM((steps, block, width), BF16), pltpu.SemaphoreType.DMA((2 * steps,))],
        compiler_params=pltpu.CompilerParams(vmem_limit_bytes=16 * MIB),
        cost_estimate=pl.CostEstimate(
            flops=2 * steps * block * width, bytes_accessed=6 * steps * block * width, transcendentals=0
        ),
        name="movers",
    )(block_list, home_pos, counts, keep, vectors)
    return outs[0], outs[1], outs[2], outs[3 : 3 + steps], outs[3 + steps :]


def sums_kernel(alive_ref, vec_ref, sums_ref):
    tile_blocks, block = alive_ref.shape
    alive = alive_ref[...]
    row = iota((tile_blocks, block), 0)
    spread = jnp.concatenate([jnp.where(row == j, alive, 0.0) for j in range(tile_blocks)], axis=1)
    sums_ref[...] = jnp.dot(spread.astype(BF16), vec_ref[...], preferred_element_type=F32)


def block_sums(alive, vectors):
    blocks, block = alive.shape
    rows, width = vectors.shape
    tile = 8
    return pl.pallas_call(
        sums_kernel,
        out_shape=jax.ShapeDtypeStruct((blocks, width), F32),
        grid=(blocks // tile,),
        in_specs=[
            pl.BlockSpec((tile, block), lambda t: (t, 0)),
            pl.BlockSpec((tile * block, width), lambda t: (t, 0)),
        ],
        out_specs=pl.BlockSpec((tile, width), lambda t: (t, 0)),
        compiler_params=pltpu.CompilerParams(vmem_limit_bytes=24 * MIB),
        cost_estimate=pl.CostEstimate(
            flops=2 * tile * rows * width, bytes_accessed=2 * rows * width, transcendentals=0
        ),
        name="block_sums",
    )(alive, vectors)


def pack_kernel(meta_ref, sums_ref, *rest):
    heads, out_ref = rest[:-1], rest[-1]
    blocks, width = sums_ref.shape
    rows = out_ref.shape[0]
    chunks = width // 128
    lane = iota((1, 128), 1)
    slots, counts = meta_ref[0:1, :], meta_ref[1:2, :]
    arrived = []
    for k, head in enumerate(heads):
        arrived.append(jnp.concatenate([head[j : j + 1, :] for j in range(chunks)], axis=1))
        slots = jnp.where(lane == blocks + k, head[chunks + 1 : chunks + 2, :], slots)
        counts = jnp.where(lane == blocks + k, head[chunks : chunks + 1, :], counts)
    spare = rows - blocks - len(heads)
    values = jnp.concatenate([sums_ref[...]] + arrived + [jnp.zeros((spare, width), F32)], axis=0)
    largest = jnp.maximum(jnp.max(jnp.abs(values), axis=1, keepdims=True), 2.0**-80)
    exponent = jnp.ceil(jnp.log2(largest) + 0.001) - 15.0
    coded = jnp.round(values * power(-exponent))
    column = jnp.concatenate(
        [jnp.broadcast_to(exponent, (rows, 128)), jnp.zeros((128 - rows, 128), F32)], axis=0
    )
    exponents = jnp.transpose(column)[0:1, :]
    extra = jnp.concatenate([slots, counts, exponents], axis=0)
    extra = jnp.concatenate([extra, jnp.zeros((3, width - 128), F32)], axis=1)
    coded = jnp.concatenate([coded[: rows - 3], extra], axis=0)
    out_ref[...] = coded.astype(jnp.int32).astype(jnp.int16)


def pack(meta, sums, heads):
    blocks, width = sums.shape
    rows = -(-(blocks + len(heads) + 3) // 8) * 8
    return pl.pallas_call(
        pack_kernel,
        out_shape=jax.ShapeDtypeStruct((rows, width), jnp.int16),
        in_specs=[VMEM] * (2 + len(heads)),
        out_specs=VMEM,
        compiler_params=pltpu.CompilerParams(vmem_limit_bytes=16 * MIB),
        cost_estimate=pl.CostEstimate(flops=8 * rows * width, bytes_accessed=6 * rows * width, transcendentals=0),
        name="pack",
    )(meta, sums, *heads)


def table_kernel(n_own, n_steps, *refs):
    own, far, old_ref = refs[:n_own], refs[n_own], refs[n_own + 1]
    row_refs = refs[n_own + 2 : n_own + 2 + n_steps]
    table_ref, norms_ref, share_ref = refs[n_own + 2 + n_steps : n_own + 5 + n_steps]
    part_refs = refs[n_own + 5 + n_steps :]
    lists, width = old_ref.shape
    rows = own[0].shape[0]
    coded = [ref[...].astype(jnp.int32) for ref in own]
    far_all = far[...].astype(jnp.int32)
    coded += [far_all[j * rows : (j + 1) * rows] for j in range(far.shape[0] // rows)]
    sources = len(coded)
    spot = iota((rows, lists), 1)
    high, low, pick_high, pick_low, hits, counts = [], [], [], [], [], []
    for values in coded:
        extra = values[rows - 3 : rows, 0:128].astype(F32)
        turned = jnp.transpose(jnp.concatenate([extra, jnp.zeros((125, 128), F32)], axis=0))
        valid = iota((rows, 1), 0) < rows - 3
        slot = jnp.where(valid, turned[0:rows, 0:1], -1.0).astype(jnp.int32)
        hit = spot == slot
        scale = power(turned[0:rows, 2:3])
        hits.append(jnp.where(hit, 1.0, 0.0).astype(BF16))
        pick_high.append(jnp.where(hit, scale * 256.0, 0.0).astype(BF16))
        pick_low.append(jnp.where(hit, scale, 0.0).astype(BF16))
        counts.append(jnp.broadcast_to(turned[0:rows, 1:2], (rows, 128)).astype(BF16))
        high.append((values >> 8).astype(F32).astype(BF16))
        low.append((values & 255).astype(F32).astype(BF16))
    totals = lax.dot_general(
        jnp.concatenate(hits, axis=0), jnp.concatenate(counts, axis=0), COL_DIMS, preferred_element_type=F32
    )
    sums = lax.dot_general(
        jnp.concatenate(pick_high + pick_low, axis=0),
        jnp.concatenate(high + low, axis=0),
        COL_DIMS,
        preferred_element_type=F32,
    )
    prior = 1.0 * PRIOR
    weight = totals[:, 0:1] + prior
    table = ((sums + prior * old_ref[...].astype(F32)) / weight).astype(BF16)
    table_ref[...] = table
    share = share_ref.shape[0]
    start = pl.multiple_of(lax.axis_index("row") * share, share)
    share_ref[...] = table_ref[pl.ds(start, share), :]
    squares = jnp.square(table.astype(F32))
    head = squares.astype(BF16)
    tail = (squares - head.astype(F32)).astype(BF16)
    ones = jnp.ones((16, width), BF16)
    norms = lax.dot_general(ones, head, ROW_DIMS, preferred_element_type=F32)
    norms = norms + lax.dot_general(ones, tail, ROW_DIMS, preferred_element_type=F32)
    norms_ref[...] = norms[0:8]
    factor = 1.0 / math.sqrt(width)
    for row_ref, part_ref in zip(row_refs, part_refs):
        dots = lax.dot_general(row_ref[...], table, ROW_DIMS, preferred_element_type=F32)
        part_ref[...] = ((2.0 * dots - norms[0:1, :]) * factor).astype(part_ref.dtype)


def make_table(n_rows, own, far, old, rows):
    lists, width = old.shape
    return pl.pallas_call(
        functools.partial(table_kernel, len(own), len(rows)),
        out_shape=[
            jax.ShapeDtypeStruct((lists, width), BF16),
            jax.ShapeDtypeStruct((8, lists), F32),
            jax.ShapeDtypeStruct((lists // n_rows, width), BF16),
        ]
        + [jax.ShapeDtypeStruct((r.shape[0], lists), BF16) for r in rows],
        in_specs=[VMEM] * (len(own) + 2 + len(rows)),
        out_specs=[VMEM] * (3 + len(rows)),
        compiler_params=pltpu.CompilerParams(vmem_limit_bytes=40 * MIB),
        cost_estimate=pl.CostEstimate(
            flops=2 * lists * width * (1000), bytes_accessed=8 * lists * width, transcendentals=0
        ),
        name="table",
    )(*own, far, old, *rows)


def turned_weights(weights):
    return jnp.transpose(jnp.broadcast_to(weights, (128, 128)))


def scores_kernel(alive_ref, norms_ref, table_ref, vec_ref, out_ref):
    tile_blocks, block = alive_ref.shape
    lists, width = table_ref.shape
    factor = 1.0 / math.sqrt(width)
    norms = norms_ref[0:1, :]
    for j in range(tile_blocks):
        at = slice(j * block, (j + 1) * block)
        dots = lax.dot_general(vec_ref[at, :], table_ref[...], ROW_DIMS, preferred_element_type=F32)
        weights = jnp.concatenate([turned_weights(alive_ref[j : j + 1, :])] * (lists // 128), axis=1)
        out_ref[at, :] = (2.0 * dots - norms) * factor * weights


def scores_of(alive, norms, table, vectors):
    blocks, block = alive.shape
    rows, width = vectors.shape
    lists = table.shape[0]
    tile = 8
    return pl.pallas_call(
        scores_kernel,
        out_shape=jax.ShapeDtypeStruct((rows, lists), F32),
        grid=(blocks // tile,),
        in_specs=[
            pl.BlockSpec((tile, block), lambda t: (t, 0)),
            pl.BlockSpec((8, lists), lambda t: (0, 0)),
            pl.BlockSpec((lists, width), lambda t: (0, 0)),
            pl.BlockSpec((tile * block, width), lambda t: (t, 0)),
        ],
        out_specs=pl.BlockSpec((tile * block, lists), lambda t: (t, 0)),
        compiler_params=pltpu.CompilerParams(vmem_limit_bytes=32 * MIB),
        cost_estimate=pl.CostEstimate(
            flops=2 * lists * rows * width, bytes_accessed=2 * rows * width + 4 * rows * lists, transcendentals=0
        ),
        name="scores",
    )(alive, norms, table, vectors)


def merge_kernel(picks_ref, alive_ref, *refs):
    steps = picks_ref.shape[0]
    parts, out_ref, held, sems = refs[:steps], refs[steps + 1], refs[steps + 2], refs[steps + 3]
    block, lists = parts[0].shape
    for k in range(steps):
        pick = picks_ref[k]

        @pl.when(pick >= 0)
        def _():
            weights = turned_weights(alive_ref[pl.ds(pick, 1), :])
            weights = jnp.concatenate([weights] * (lists // 128), axis=1)
            held[k] = parts[k][...].astype(F32) * weights
            start = pl.multiple_of(pick * block, block)
            pltpu.make_async_copy(held.at[k], out_ref.at[pl.ds(start, block), :], sems.at[k]).start()

    for k in range(steps):
        pick = picks_ref[k]

        @pl.when(pick >= 0)
        def _():
            start = pl.multiple_of(pick * block, block)
            pltpu.make_async_copy(held.at[k], out_ref.at[pl.ds(start, block), :], sems.at[k]).wait()


def merge(picks, alive, parts, scores):
    steps = len(parts)
    block, lists = parts[0].shape
    return pl.pallas_call(
        merge_kernel,
        out_shape=jax.ShapeDtypeStruct(scores.shape, scores.dtype),
        in_specs=[SMEM, VMEM] + [VMEM] * steps + [HBM],
        out_specs=HBM,
        scratch_shapes=[pltpu.VMEM((steps, block, lists), F32), pltpu.SemaphoreType.DMA((steps,))],
        input_output_aliases={2 + steps: 0},
        compiler_params=pltpu.CompilerParams(vmem_limit_bytes=16 * MIB),
        cost_estimate=pl.CostEstimate(
            flops=2 * steps * block * lists, bytes_accessed=6 * steps * block * lists, transcendentals=0
        ),
        name="merge",
    )(picks, alive, *parts, scores)


def local(vectors, keep_bits, counts, block_list, home_pos, old_centroids):
    n_groups = lax.axis_size("grp")
    n_rows = lax.axis_size("row")
    blocks = counts.shape[0]
    block = vectors.shape[0] // blocks
    lists_group = old_centroids.shape[0]
    keep = keep_bits.reshape(blocks, block)
    there = [[(i, peer(i, k, n_groups)) for i in range(n_groups)] for k in range(1, n_groups)]
    back = [[(j, i) for i, j in pairs] for pairs in there]

    alive, meta, picks, heads, rows = movers(
        n_groups, lists_group, block_list, home_pos, counts, keep, vectors
    )
    heads = [lax.ppermute(x, "grp", pairs) for x, pairs in zip(heads, there)]
    rows = [lax.ppermute(x, "grp", pairs) for x, pairs in zip(rows, there)]
    sums = block_sums(alive, vectors)
    mine = pack(meta, sums, heads)
    chips = n_rows // 2
    own = [mine]
    for k in range(chips - 1, 0, -1):
        pairs = [(i, 2 * peer(i // 2, k, chips) + i % 2) for i in range(n_rows)]
        own.append(lax.ppermute(mine, "row", pairs))
    far = lax.ppermute(jnp.concatenate(own, axis=0), "row", [(i, i ^ 1) for i in range(n_rows)])
    table, norms, share, *parts = make_table(n_rows, own, far, old_centroids, rows)
    parts = [lax.ppermute(x, "grp", pairs) for x, pairs in zip(parts, back)]
    scores = scores_of(alive, norms, table, vectors)
    scores = merge(picks, alive, parts, scores)
    return (share, scores)


def solution(mesh):
    in_specs = (
        P(("grp", "row"), None),
        P(("grp", "row")),
        P(("grp", "row")),
        P(),
        P(),
        P("grp", None),
    )
    out_specs = (P(("grp", "row"), None), P(("grp", "row"), None))
    return jax.shard_map(local, mesh=mesh, in_specs=in_specs, out_specs=out_specs, check_vma=False)
```

```python
import functools
import math

import jax
import jax.numpy as jnp
from jax import lax
from jax.experimental import pallas as pl
from jax.experimental.pallas import tpu as pltpu
from jax.sharding import PartitionSpec as P

PRIOR = 16
MIB = 1 << 20
F32 = jnp.float32
BF16 = jnp.bfloat16
I16 = jnp.int16
I32 = jnp.int32
ROW_DIMS = (((1,), (1,)), ((), ()))
COL_DIMS = (((0,), (0,)), ((), ()))
VMEM = pl.BlockSpec(memory_space=pltpu.VMEM)
SMEM = pl.BlockSpec(memory_space=pltpu.SMEM)
HBM = pl.BlockSpec(memory_space=pltpu.HBM)


def peer(index, step, size):
    if size & (size - 1) == 0:
        return index ^ step
    return (index + step) % size


def power(exponent):
    return jnp.exp2(exponent).astype(BF16).astype(F32)


def iota(shape, dim):
    return lax.broadcasted_iota(I32, shape, dim)


def shaped(shape, dtype):
    return jax.ShapeDtypeStruct(shape, dtype)


def params(mib):
    return pltpu.CompilerParams(vmem_limit_bytes=mib * MIB)


def cost(flops, size):
    return pl.CostEstimate(flops=flops, bytes_accessed=size, transcendentals=0)


def in_hbm(array):
    return pltpu.with_memory_space_constraint(array, pltpu.HBM)


def as_lanes(column):
    rows = column.shape[0]
    wide = jnp.broadcast_to(column, (rows, 128))
    return jnp.transpose(jnp.concatenate([wide, jnp.zeros((128 - rows, 128), F32)], axis=0))[0:1, :]


def coded_rows(values):
    largest = jnp.maximum(jnp.max(jnp.abs(values), axis=1, keepdims=True), 2.0**-80)
    exponent = jnp.ceil(jnp.log2(largest) + 0.001) - 15.0
    return jnp.round(values * power(-exponent)).astype(I32), exponent


def turned_weights(weights):
    return jnp.transpose(jnp.broadcast_to(weights, (128, 128)))


def movers_kernel(n_groups, lists_group, list_ref, pos_ref, counts_ref, keep_ref, vec_ref, *refs):
    steps = n_groups - 1
    alive_ref, meta_ref, picks_ref = refs[:3]
    head_refs, row_refs = refs[3 : 3 + steps], refs[3 + steps : 3 + 2 * steps]
    lists, pos, fill, held, sems = refs[3 + 2 * steps :]
    loads = [
        pltpu.make_async_copy(src, dst, sems.at[steps + i])
        for i, (src, dst) in enumerate([(list_ref, lists), (pos_ref, pos), (counts_ref, fill), (keep_ref, held)])
    ]
    for load in loads:
        load.start()
    blocks, block = keep_ref.shape
    group = lax.axis_index("grp")
    base = (group * lax.axis_size("row") + lax.axis_index("row")) * blocks
    lane = iota((1, block), 1)
    row = iota((blocks, block), 0)
    slots = jnp.full((1, block), -1, I32)
    filled = jnp.zeros((blocks, block), I32)
    picks = [jnp.int32(-1)] * steps
    homes = [jnp.int32(-1)] * steps
    for load in loads:
        load.wait()
    for b in range(blocks):
        home = pos[lists[base + b]]
        home_group = home // lists_group
        slot = home - home_group * lists_group
        slots = jnp.where((lane == b) & (home_group == group), slot, slots)
        for k in range(steps):
            hit = home_group == peer(group, k + 1, n_groups)
            picks[k] = jnp.where(hit, b, picks[k])
            homes[k] = jnp.where(hit, slot, homes[k])
    fetches = []
    for k in range(steps):
        picks_ref[k] = picks[k]
        start = pl.multiple_of(jnp.maximum(picks[k], 0) * block, block)
        fetches.append(pltpu.make_async_copy(vec_ref.at[pl.ds(start, block), :], row_refs[k], sems.at[k]))
        fetches[k].start()
    for b in range(blocks):
        filled = jnp.where(row == b, fill[b], filled)
    alive = held[...].astype(F32) * (iota((blocks, block), 1) < filled).astype(F32)
    alive_ref[...] = alive
    ones = jnp.ones((8, block), BF16)
    block_counts = lax.dot_general(ones, alive.astype(BF16), ROW_DIMS, preferred_element_type=F32)
    meta_ref[...] = jnp.zeros_like(meta_ref)
    meta_ref[0:1, :] = slots.astype(F32)
    meta_ref[1:2, 0:blocks] = block_counts[0:1, :]
    for k in range(steps):
        fetches[k].wait()
        weights = alive_ref[pl.ds(jnp.maximum(picks[k], 0), 1), :]
        wide = jnp.broadcast_to(weights, (16, block)).astype(BF16)
        total = jnp.dot(wide, row_refs[k][...], preferred_element_type=F32)
        chunks = total.shape[1] // 128
        for j in range(chunks):
            head_refs[k][j : j + 1, :] = total[0:1, j * 128 : (j + 1) * 128]
        head_refs[k][chunks : chunks + 8, :] = jnp.concatenate(
            [
                jnp.broadcast_to(jnp.sum(weights, axis=1, keepdims=True), (1, 128)),
                jnp.broadcast_to(homes[k].astype(F32), (1, 128)),
                jnp.zeros((6, 128), F32),
            ],
            axis=0,
        )


def movers(n_groups, lists_group, block_list, home_pos, counts, keep, vectors):
    steps = n_groups - 1
    blocks, block = keep.shape
    width = vectors.shape[1]
    outs = pl.pallas_call(
        functools.partial(movers_kernel, n_groups, lists_group),
        out_shape=[shaped((blocks, block), F32), shaped((8, block), F32), shaped((steps,), I32)]
        + [shaped((width // 128 + 8, 128), F32)] * steps
        + [shaped((block, width), BF16)] * steps,
        in_specs=[HBM] * 5,
        out_specs=[VMEM, VMEM, SMEM] + [VMEM] * (2 * steps),
        scratch_shapes=[
            pltpu.SMEM(block_list.shape, I32),
            pltpu.SMEM(home_pos.shape, I32),
            pltpu.SMEM(counts.shape, I32),
            pltpu.VMEM(keep.shape, I32),
            pltpu.SemaphoreType.DMA((steps + 4,)),
        ],
        compiler_params=params(8),
        cost_estimate=cost(2 * steps * block * width, 6 * steps * block * width),
        name="movers",
    )(*map(in_hbm, (block_list, home_pos, counts, keep, vectors)))
    return outs[0], outs[1], outs[2], outs[3 : 3 + steps], outs[3 + steps :]


def sums_kernel(alive_ref, vec_ref, sums_ref):
    blocks, block = alive_ref.shape
    tile = 8
    row = iota((tile, block), 0)
    for t in range(blocks // tile):
        alive = alive_ref[t * tile : (t + 1) * tile, :]
        spread = jnp.concatenate([jnp.where(row == j, alive, 0.0) for j in range(tile)], axis=1)
        rows = vec_ref[t * tile * block : (t + 1) * tile * block, :]
        sums_ref[t * tile : (t + 1) * tile, :] = jnp.dot(spread.astype(BF16), rows, preferred_element_type=F32)


def block_sums(alive, vectors):
    blocks = alive.shape[0]
    rows, width = vectors.shape
    return pl.pallas_call(
        sums_kernel,
        out_shape=shaped((blocks, width), F32),
        in_specs=[VMEM] * 2,
        out_specs=VMEM,
        compiler_params=params(16),
        cost_estimate=cost(16 * rows * width, 2 * rows * width),
        name="block_sums",
    )(alive, vectors)


def pack_kernel(meta_ref, sums_ref, *refs):
    heads, out_ref = refs[:-1], refs[-1]
    blocks, width = sums_ref.shape
    rows = out_ref.shape[0]
    chunks = width // 128
    lane = iota((1, 128), 1)
    slots, counts = meta_ref[0:1, :], meta_ref[1:2, :]
    arrived = []
    for k, head in enumerate(heads):
        arrived.append(jnp.concatenate([head[j : j + 1, :] for j in range(chunks)], axis=1))
        slots = jnp.where(lane == blocks + k, head[chunks + 1 : chunks + 2, :], slots)
        counts = jnp.where(lane == blocks + k, head[chunks : chunks + 1, :], counts)
    spare = rows - blocks - len(heads)
    coded, exponent = coded_rows(
        jnp.concatenate([sums_ref[...]] + arrived + [jnp.zeros((spare, width), F32)], axis=0)
    )
    extra = jnp.concatenate([slots, counts, as_lanes(exponent)], axis=0).astype(I32)
    extra = jnp.concatenate([extra, jnp.zeros((3, width - 128), I32)], axis=1)
    out_ref[...] = jnp.concatenate([coded[: rows - 3], extra], axis=0).astype(I16)


def pack(meta, sums, heads):
    blocks, width = sums.shape
    rows = blocks + -(-(len(heads) + 3) // 8) * 8
    return pl.pallas_call(
        pack_kernel,
        out_shape=shaped((rows, width), I16),
        in_specs=[VMEM] * (2 + len(heads)),
        out_specs=VMEM,
        compiler_params=params(8),
        cost_estimate=cost(8 * rows * width, 6 * rows * width),
        name="pack",
    )(meta, sums, *heads)


def add_up(sources, blocks, lists):
    rows = sources[0].shape[0]

    def lanes(which, first, last):
        parts = [x[rows - 3 + which : rows - 2 + which, first:last].astype(F32) for x in sources]
        return jnp.concatenate(parts, axis=1)

    picks_high, picks_low, high, low, hits, counts = [], [], [], [], [], []
    for first, last in ((0, blocks), (blocks, rows)):
        values = jnp.concatenate([x[first:last] for x in sources], axis=0)
        hit = iota((lists, values.shape[0]), 0) == lanes(0, first, last).astype(I32)
        scale = power(lanes(2, first, last))
        hits.append(jnp.where(hit, 1.0, 0.0).astype(BF16))
        picks_high.append(jnp.where(hit, scale * 256.0, 0.0).astype(BF16))
        picks_low.append(jnp.where(hit, scale, 0.0).astype(BF16))
        counts.append(jnp.broadcast_to(lanes(1, first, last), (128, values.shape[0])).astype(BF16))
        high.append((values >> 8).astype(F32).astype(BF16))
        low.append((values & 255).astype(F32).astype(BF16))
    totals = lax.dot_general(
        jnp.concatenate(hits, axis=1), jnp.concatenate(counts, axis=1), ROW_DIMS, preferred_element_type=F32
    )
    sums = jnp.dot(
        jnp.concatenate(picks_high + picks_low, axis=1),
        jnp.concatenate(high + low, axis=0),
        preferred_element_type=F32,
    )
    return sums, totals


def prior_kernel(blocks, mine_ref, old_ref, sums_ref, totals_ref):
    lists = old_ref.shape[0]
    prior = 1.0 * PRIOR
    sums, totals = add_up([mine_ref[...].astype(I32)], blocks, lists)
    sums_ref[...] = sums + prior * old_ref[...].astype(F32)
    totals_ref[...] = totals + prior


def with_prior(blocks, mine, old):
    lists, width = old.shape
    return pl.pallas_call(
        functools.partial(prior_kernel, blocks),
        out_shape=[shaped((lists, width), F32), shaped((lists, 128), F32)],
        in_specs=[VMEM] * 2,
        out_specs=[VMEM] * 2,
        compiler_params=params(16),
        cost_estimate=cost(20000 * lists * width, 8 * lists * width),
        name="prior",
    )(mine, old)


def table_kernel(blocks, n_near, *refs):
    near, far = refs[:n_near], refs[n_near]
    sums_ref, totals_ref, table_ref, norms_ref, share_ref = refs[n_near + 1 :]
    lists, width = sums_ref.shape
    rows = near[0].shape[0]
    sources = [ref[...].astype(I32) for ref in near]
    sources += [far[j * rows : (j + 1) * rows, :].astype(I32) for j in range(n_near + 1)]
    sums, totals = add_up(sources, blocks, lists)
    totals = totals_ref[:, 0:1] + totals[:, 0:1]
    table = ((sums_ref[...] + sums) * (1.0 / totals)).astype(BF16)
    table_ref[...] = table
    share = share_ref.shape[0]
    start = pl.multiple_of(lax.axis_index("row") * share, share)
    share_ref[...] = table_ref[pl.ds(start, share), :]
    squares = jnp.square(table.astype(F32))
    partial = squares[:, 0:128]
    for j in range(1, width // 128):
        partial = partial + squares[:, j * 128 : (j + 1) * 128]
    ones = jnp.ones((16, 128), BF16)
    norms = jnp.zeros((16, lists), F32)
    for _ in range(3):
        piece = partial.astype(BF16)
        partial = partial - piece.astype(F32)
        norms = norms + lax.dot_general(ones, piece, ROW_DIMS, preferred_element_type=F32)
    norms_ref[...] = norms[0:8] * (1.0 / math.sqrt(width))


def make_table(n_rows, blocks, near, far, sums, totals):
    lists, width = sums.shape
    return pl.pallas_call(
        functools.partial(table_kernel, blocks, len(near)),
        out_shape=[shaped((lists, width), BF16), shaped((8, lists), F32), shaped((lists // n_rows, width), BF16)],
        in_specs=[VMEM] * (len(near) + 3),
        out_specs=[VMEM] * 3,
        compiler_params=params(24),
        cost_estimate=cost(2000 * lists * width, 8 * lists * width),
        name="table",
    )(*near, far, sums, totals)


def parts_kernel(norms_ref, table_ref, *refs):
    steps = len(refs) // 2
    factor = 1.0 / math.sqrt(table_ref.shape[1])
    norms = norms_ref[0:1, :]
    for row_ref, part_ref in zip(refs[:steps], refs[steps:]):
        dots = lax.dot_general(row_ref[...], table_ref[...], ROW_DIMS, preferred_element_type=F32)
        part_ref[...] = (dots * (2.0 * factor) - norms).astype(part_ref.dtype)


def parts_of(norms, table, rows):
    lists, width = table.shape
    block = rows[0].shape[0]
    return pl.pallas_call(
        parts_kernel,
        out_shape=[shaped((block, lists), BF16)] * len(rows),
        in_specs=[VMEM] * (2 + len(rows)),
        out_specs=[VMEM] * len(rows),
        compiler_params=params(16),
        cost_estimate=cost(2 * len(rows) * block * lists * width, 2 * lists * width),
        name="parts",
    )(norms, table, *rows)


def scores_kernel(alive_ref, norms_ref, table_ref, vec_ref, out_ref, held, sems):
    blocks, block = alive_ref.shape
    lists, width = table_ref.shape
    factor = 1.0 / math.sqrt(width)
    norms = norms_ref[0:1, :]
    table = table_ref[...]
    tile = 4
    stores = []
    for t in range(blocks // tile):
        span = slice(t * tile * block, (t + 1) * tile * block)
        dots = lax.dot_general(vec_ref[span, :], table, ROW_DIMS, preferred_element_type=F32)
        for j in range(tile):
            b = t * tile + j
            weights = jnp.concatenate([turned_weights(alive_ref[b : b + 1, :])] * (lists // 128), axis=1)
            part = dots[j * block : (j + 1) * block, :]
            held[b * block : (b + 1) * block, :] = (part * (2.0 * factor) - norms) * weights
        stores.append(pltpu.make_async_copy(held.at[span, :], out_ref.at[span, :], sems.at[t]))
        stores[t].start()
    for store in stores:
        store.wait()


def scores_of(alive, norms, table, vectors):
    blocks = alive.shape[0]
    rows, width = vectors.shape
    lists = table.shape[0]
    return pl.pallas_call(
        scores_kernel,
        out_shape=shaped((rows, lists), F32),
        in_specs=[VMEM] * 4,
        out_specs=HBM,
        scratch_shapes=[pltpu.VMEM((rows, lists), F32), pltpu.SemaphoreType.DMA((blocks // 4,))],
        compiler_params=params(24),
        cost_estimate=cost(2 * lists * rows * width, 4 * rows * lists),
        name="scores",
    )(alive, norms, table, vectors)


def merge_kernel(picks_ref, alive_ref, *refs):
    steps = picks_ref.shape[0]
    parts, out_ref, held, sems = refs[:steps], refs[steps + 1], refs[steps + 2], refs[steps + 3]
    block, lists = parts[0].shape

    def store(k):
        start = pl.multiple_of(picks_ref[k] * block, block)
        return pltpu.make_async_copy(held.at[k], out_ref.at[pl.ds(start, block), :], sems.at[k])

    for k in range(steps):

        @pl.when(picks_ref[k] >= 0)
        def _():
            weights = turned_weights(alive_ref[pl.ds(picks_ref[k], 1), :])
            weights = jnp.concatenate([weights] * (lists // 128), axis=1)
            held[k] = parts[k][...].astype(F32) * weights
            store(k).start()

    for k in range(steps):

        @pl.when(picks_ref[k] >= 0)
        def _():
            store(k).wait()


def merge(picks, alive, parts, scores):
    steps = len(parts)
    block, lists = parts[0].shape
    return pl.pallas_call(
        merge_kernel,
        out_shape=shaped(scores.shape, scores.dtype),
        in_specs=[SMEM, VMEM] + [VMEM] * steps + [HBM],
        out_specs=HBM,
        scratch_shapes=[pltpu.VMEM((steps, block, lists), F32), pltpu.SemaphoreType.DMA((steps,))],
        input_output_aliases={2 + steps: 0},
        compiler_params=params(8),
        cost_estimate=cost(2 * steps * block * lists, 6 * steps * block * lists),
        name="merge",
    )(picks, alive, *parts, scores)


def local(vectors, keep_bits, counts, block_list, home_pos, old_centroids):
    n_groups = lax.axis_size("grp")
    n_rows = lax.axis_size("row")
    blocks = counts.shape[0]
    block = vectors.shape[0] // blocks
    lists_group = old_centroids.shape[0]
    keep = keep_bits.reshape(blocks, block)
    there = [[(i, peer(i, k, n_groups)) for i in range(n_groups)] for k in range(1, n_groups)]
    back = [[(j, i) for i, j in pairs] for pairs in there]
    chips = n_rows // 2
    along = [[(i, 2 * peer(i // 2, k, chips) + i % 2) for i in range(n_rows)] for k in range(1, chips)]
    cores = [(i, i ^ 1) for i in range(n_rows)]

    alive, meta, picks, heads, rows = movers(n_groups, lists_group, block_list, home_pos, counts, keep, vectors)
    heads = [lax.ppermute(x, "grp", pairs) for x, pairs in zip(heads, there)]
    mine = pack(meta, block_sums(alive, vectors), heads)
    mine, *rows = lax.optimization_barrier((mine, *rows))
    rows = [lax.ppermute(x, "grp", pairs) for x, pairs in zip(rows, there)]
    near = [lax.ppermute(mine, "row", pairs) for pairs in along]
    sums, totals = with_prior(blocks, mine, old_centroids)
    far = lax.ppermute(jnp.concatenate([mine] + near, axis=0), "row", cores)
    table, norms, share = make_table(n_rows, blocks, near, far, sums, totals)
    parts = parts_of(norms, table, rows)
    parts = [lax.ppermute(x, "grp", pairs) for x, pairs in zip(parts, back)]
    scores = scores_of(alive, norms, table, vectors)
    scores = merge(picks, alive, parts, scores)
    return (share, scores)


def solution(mesh):
    in_specs = (
        P(("grp", "row"), None),
        P(("grp", "row")),
        P(("grp", "row")),
        P(),
        P(),
        P("grp", None),
    )
    out_specs = (P(("grp", "row"), None), P(("grp", "row"), None))
    return jax.shard_map(local, mesh=mesh, in_specs=in_specs, out_specs=out_specs, check_vma=False)
```

```python
import functools
import math

import jax
import jax.numpy as jnp
from jax import lax
from jax.experimental import pallas as pl
from jax.experimental.pallas import tpu as pltpu
from jax.sharding import PartitionSpec as P

PRIOR = 16
MIB = 1 << 20
F32 = jnp.float32
BF16 = jnp.bfloat16
I16 = jnp.int16
I32 = jnp.int32
ROW_DIMS = (((1,), (1,)), ((), ()))
COL_DIMS = (((0,), (0,)), ((), ()))
VMEM = pl.BlockSpec(memory_space=pltpu.VMEM)
SMEM = pl.BlockSpec(memory_space=pltpu.SMEM)
HBM = pl.BlockSpec(memory_space=pltpu.HBM)


def peer(index, step, size):
    if size & (size - 1) == 0:
        return index ^ step
    return (index + step) % size


def power(exponent):
    return jnp.exp2(exponent).astype(BF16).astype(F32)


def iota(shape, dim):
    return lax.broadcasted_iota(I32, shape, dim)


def shaped(shape, dtype):
    return jax.ShapeDtypeStruct(shape, dtype)


def params(mib):
    return pltpu.CompilerParams(vmem_limit_bytes=mib * MIB)


def cost(flops, size):
    return pl.CostEstimate(flops=flops, bytes_accessed=size, transcendentals=0)


def in_hbm(array):
    return pltpu.with_memory_space_constraint(array, pltpu.HBM)


def as_lanes(column):
    rows = column.shape[0]
    wide = jnp.broadcast_to(column, (rows, 128))
    return jnp.transpose(jnp.concatenate([wide, jnp.zeros((128 - rows, 128), F32)], axis=0))[0:1, :]


def coded_rows(values):
    largest = jnp.maximum(jnp.max(jnp.abs(values), axis=1, keepdims=True), 2.0**-80)
    exponent = jnp.ceil(jnp.log2(largest) + 0.001) - 15.0
    return jnp.round(values * power(-exponent)).astype(I32), exponent


def turned_weights(weights):
    return jnp.transpose(jnp.broadcast_to(weights, (128, 128)))


def movers_kernel(n_groups, lists_group, list_ref, pos_ref, counts_ref, keep_ref, vec_ref, *refs):
    steps = n_groups - 1
    alive_ref, meta_ref, picks_ref = refs[:3]
    head_refs, row_refs = refs[3 : 3 + steps], refs[3 + steps : 3 + 2 * steps]
    lists, pos, fill, held, sems = refs[3 + 2 * steps :]
    loads = [
        pltpu.make_async_copy(src, dst, sems.at[steps + i])
        for i, (src, dst) in enumerate([(list_ref, lists), (pos_ref, pos), (counts_ref, fill), (keep_ref, held)])
    ]
    for load in loads:
        load.start()
    blocks, block = keep_ref.shape
    group = lax.axis_index("grp")
    base = (group * lax.axis_size("row") + lax.axis_index("row")) * blocks
    lane = iota((1, block), 1)
    row = iota((blocks, block), 0)
    slots = jnp.full((1, block), -1, I32)
    filled = jnp.zeros((blocks, block), I32)
    picks = [jnp.int32(-1)] * steps
    homes = [jnp.int32(-1)] * steps
    for load in loads:
        load.wait()
    for b in range(blocks):
        home = pos[lists[base + b]]
        home_group = home // lists_group
        slot = home - home_group * lists_group
        slots = jnp.where((lane == b) & (home_group == group), slot, slots)
        for k in range(steps):
            hit = home_group == peer(group, k + 1, n_groups)
            picks[k] = jnp.where(hit, b, picks[k])
            homes[k] = jnp.where(hit, slot, homes[k])
    fetches = []
    for k in range(steps):
        picks_ref[k] = picks[k]
        start = pl.multiple_of(jnp.maximum(picks[k], 0) * block, block)
        fetches.append(pltpu.make_async_copy(vec_ref.at[pl.ds(start, block), :], row_refs[k], sems.at[k]))
        fetches[k].start()
    for b in range(blocks):
        filled = jnp.where(row == b, fill[b], filled)
    alive = held[...].astype(F32) * (iota((blocks, block), 1) < filled).astype(F32)
    alive_ref[...] = alive
    ones = jnp.ones((8, block), BF16)
    block_counts = lax.dot_general(ones, alive.astype(BF16), ROW_DIMS, preferred_element_type=F32)
    meta_ref[...] = jnp.zeros_like(meta_ref)
    meta_ref[0:1, :] = slots.astype(F32)
    meta_ref[1:2, 0:blocks] = block_counts[0:1, :]
    for k in range(steps):
        fetches[k].wait()
        weights = alive_ref[pl.ds(jnp.maximum(picks[k], 0), 1), :]
        wide = jnp.broadcast_to(weights, (16, block)).astype(BF16)
        total = jnp.dot(wide, row_refs[k][...], preferred_element_type=F32)
        chunks = total.shape[1] // 128
        for j in range(chunks):
            head_refs[k][j : j + 1, :] = total[0:1, j * 128 : (j + 1) * 128]
        head_refs[k][chunks : chunks + 8, :] = jnp.concatenate(
            [
                jnp.broadcast_to(jnp.sum(weights, axis=1, keepdims=True), (1, 128)),
                jnp.broadcast_to(homes[k].astype(F32), (1, 128)),
                jnp.zeros((6, 128), F32),
            ],
            axis=0,
        )


def movers(n_groups, lists_group, block_list, home_pos, counts, keep, vectors):
    steps = n_groups - 1
    blocks, block = keep.shape
    width = vectors.shape[1]
    outs = pl.pallas_call(
        functools.partial(movers_kernel, n_groups, lists_group),
        out_shape=[shaped((blocks, block), F32), shaped((8, block), F32), shaped((steps,), I32)]
        + [shaped((width // 128 + 8, 128), F32)] * steps
        + [shaped((block, width), BF16)] * steps,
        in_specs=[HBM] * 5,
        out_specs=[VMEM, VMEM, SMEM] + [VMEM] * (2 * steps),
        scratch_shapes=[
            pltpu.SMEM(block_list.shape, I32),
            pltpu.SMEM(home_pos.shape, I32),
            pltpu.SMEM(counts.shape, I32),
            pltpu.VMEM(keep.shape, I32),
            pltpu.SemaphoreType.DMA((steps + 4,)),
        ],
        compiler_params=params(8),
        cost_estimate=cost(2 * steps * block * width, 6 * steps * block * width),
        name="movers",
    )(*map(in_hbm, (block_list, home_pos, counts, keep, vectors)))
    return outs[0], outs[1], outs[2], outs[3 : 3 + steps], outs[3 + steps :]


def sums_kernel(alive_ref, vec_ref, sums_ref):
    blocks, block = alive_ref.shape
    tile = 8
    row = iota((tile, block), 0)
    for t in range(blocks // tile):
        alive = alive_ref[t * tile : (t + 1) * tile, :]
        spread = jnp.concatenate([jnp.where(row == j, alive, 0.0) for j in range(tile)], axis=1)
        rows = vec_ref[t * tile * block : (t + 1) * tile * block, :]
        sums_ref[t * tile : (t + 1) * tile, :] = jnp.dot(spread.astype(BF16), rows, preferred_element_type=F32)


def block_sums(alive, vectors):
    blocks = alive.shape[0]
    rows, width = vectors.shape
    return pl.pallas_call(
        sums_kernel,
        out_shape=shaped((blocks, width), F32),
        in_specs=[VMEM] * 2,
        out_specs=VMEM,
        compiler_params=params(16),
        cost_estimate=cost(16 * rows * width, 2 * rows * width),
        name="block_sums",
    )(alive, vectors)


def pack_kernel(meta_ref, sums_ref, *refs):
    heads, out_ref = refs[:-1], refs[-1]
    blocks, width = sums_ref.shape
    rows = out_ref.shape[0]
    chunks = width // 128
    lane = iota((1, 128), 1)
    slots, counts = meta_ref[0:1, :], meta_ref[1:2, :]
    arrived = []
    for k, head in enumerate(heads):
        arrived.append(jnp.concatenate([head[j : j + 1, :] for j in range(chunks)], axis=1))
        slots = jnp.where(lane == blocks + k, head[chunks + 1 : chunks + 2, :], slots)
        counts = jnp.where(lane == blocks + k, head[chunks : chunks + 1, :], counts)
    spare = rows - blocks - len(heads)
    coded, exponent = coded_rows(
        jnp.concatenate([sums_ref[...]] + arrived + [jnp.zeros((spare, width), F32)], axis=0)
    )
    extra = jnp.concatenate([slots, counts, as_lanes(exponent)], axis=0).astype(I32)
    extra = jnp.concatenate([extra, jnp.zeros((3, width - 128), I32)], axis=1)
    out_ref[...] = jnp.concatenate([coded[: rows - 3], extra], axis=0).astype(I16)


def pack(meta, sums, heads):
    blocks, width = sums.shape
    rows = blocks + -(-(len(heads) + 3) // 8) * 8
    return pl.pallas_call(
        pack_kernel,
        out_shape=shaped((rows, width), I16),
        in_specs=[VMEM] * (2 + len(heads)),
        out_specs=VMEM,
        compiler_params=params(8),
        cost_estimate=cost(8 * rows * width, 6 * rows * width),
        name="pack",
    )(meta, sums, *heads)


def add_up(sources, blocks, lists):
    rows = sources[0].shape[0]

    def lanes(which, first, last):
        parts = [x[rows - 3 + which : rows - 2 + which, first:last].astype(F32) for x in sources]
        return jnp.concatenate(parts, axis=1)

    picks_high, picks_low, high, low, hits, counts = [], [], [], [], [], []
    for first, last in ((0, blocks), (blocks, rows)):
        values = jnp.concatenate([x[first:last] for x in sources], axis=0)
        hit = iota((lists, values.shape[0]), 0) == lanes(0, first, last).astype(I32)
        scale = power(lanes(2, first, last))
        hits.append(jnp.where(hit, 1.0, 0.0).astype(BF16))
        picks_high.append(jnp.where(hit, scale * 256.0, 0.0).astype(BF16))
        picks_low.append(jnp.where(hit, scale, 0.0).astype(BF16))
        counts.append(jnp.broadcast_to(lanes(1, first, last), (128, values.shape[0])).astype(BF16))
        high.append((values >> 8).astype(F32).astype(BF16))
        low.append((values & 255).astype(F32).astype(BF16))
    totals = lax.dot_general(
        jnp.concatenate(hits, axis=1), jnp.concatenate(counts, axis=1), ROW_DIMS, preferred_element_type=F32
    )
    sums = jnp.dot(
        jnp.concatenate(picks_high + picks_low, axis=1),
        jnp.concatenate(high + low, axis=0),
        preferred_element_type=F32,
    )
    return sums, totals


def prior_kernel(blocks, mine_ref, old_ref, sums_ref, totals_ref):
    lists = old_ref.shape[0]
    prior = 1.0 * PRIOR
    sums, totals = add_up([mine_ref[...].astype(I32)], blocks, lists)
    sums_ref[...] = sums + prior * old_ref[...].astype(F32)
    totals_ref[...] = totals + prior


def with_prior(blocks, mine, old):
    lists, width = old.shape
    return pl.pallas_call(
        functools.partial(prior_kernel, blocks),
        out_shape=[shaped((lists, width), F32), shaped((lists, 128), F32)],
        in_specs=[VMEM] * 2,
        out_specs=[VMEM] * 2,
        compiler_params=params(16),
        cost_estimate=cost(20000 * lists * width, 8 * lists * width),
        name="prior",
    )(mine, old)


def table_kernel(blocks, n_near, *refs):
    near, far = refs[:n_near], refs[n_near]
    sums_ref, totals_ref, table_ref, norms_ref, share_ref = refs[n_near + 1 :]
    lists, width = sums_ref.shape
    rows = near[0].shape[0]
    sources = [ref[...].astype(I32) for ref in near]
    sources += [far[j * rows : (j + 1) * rows, :].astype(I32) for j in range(n_near + 1)]
    sums, totals = add_up(sources, blocks, lists)
    totals = totals_ref[:, 0:1] + totals[:, 0:1]
    table = ((sums_ref[...] + sums) * (1.0 / totals)).astype(BF16)
    table_ref[...] = table
    share = share_ref.shape[0]
    start = pl.multiple_of(lax.axis_index("row") * share, share)
    share_ref[...] = table_ref[pl.ds(start, share), :]
    squares = jnp.square(table.astype(F32))
    partial = squares[:, 0:128]
    for j in range(1, width // 128):
        partial = partial + squares[:, j * 128 : (j + 1) * 128]
    ones = jnp.ones((16, 128), BF16)
    norms = jnp.zeros((16, lists), F32)
    for _ in range(3):
        piece = partial.astype(BF16)
        partial = partial - piece.astype(F32)
        norms = norms + lax.dot_general(ones, piece, ROW_DIMS, preferred_element_type=F32)
    norms_ref[...] = norms[0:8] * (1.0 / math.sqrt(width))


def make_table(n_rows, blocks, near, far, sums, totals):
    lists, width = sums.shape
    return pl.pallas_call(
        functools.partial(table_kernel, blocks, len(near)),
        out_shape=[shaped((lists, width), BF16), shaped((8, lists), F32), shaped((lists // n_rows, width), BF16)],
        in_specs=[VMEM] * (len(near) + 3),
        out_specs=[VMEM] * 3,
        compiler_params=params(24),
        cost_estimate=cost(2000 * lists * width, 8 * lists * width),
        name="table",
    )(*near, far, sums, totals)


def parts_kernel(norms_ref, table_ref, *refs):
    steps = len(refs) // 2
    factor = 1.0 / math.sqrt(table_ref.shape[1])
    norms = norms_ref[0:1, :]
    for row_ref, part_ref in zip(refs[:steps], refs[steps:]):
        dots = lax.dot_general(row_ref[...], table_ref[...], ROW_DIMS, preferred_element_type=F32)
        part_ref[...] = (dots * (2.0 * factor) - norms).astype(part_ref.dtype)


def parts_of(norms, table, rows):
    lists, width = table.shape
    block = rows[0].shape[0]
    return pl.pallas_call(
        parts_kernel,
        out_shape=[shaped((block, lists), BF16)] * len(rows),
        in_specs=[VMEM] * (2 + len(rows)),
        out_specs=[VMEM] * len(rows),
        compiler_params=params(16),
        cost_estimate=cost(2 * len(rows) * block * lists * width, 2 * lists * width),
        name="parts",
    )(norms, table, *rows)


def scores_kernel(alive_ref, norms_ref, table_ref, vec_ref, out_ref, held, sems):
    blocks, block = alive_ref.shape
    lists, width = table_ref.shape
    factor = 1.0 / math.sqrt(width)
    norms = norms_ref[0:1, :]
    table = table_ref[...]
    tile = 4
    stores = []
    for t in range(blocks // tile):
        span = slice(t * tile * block, (t + 1) * tile * block)
        dots = lax.dot_general(vec_ref[span, :], table, ROW_DIMS, preferred_element_type=F32)
        for j in range(tile):
            b = t * tile + j
            weights = jnp.concatenate([turned_weights(alive_ref[b : b + 1, :])] * (lists // 128), axis=1)
            part = dots[j * block : (j + 1) * block, :]
            held[b * block : (b + 1) * block, :] = (part * (2.0 * factor) - norms) * weights
        stores.append(pltpu.make_async_copy(held.at[span, :], out_ref.at[span, :], sems.at[t]))
        stores[t].start()
    for store in stores:
        store.wait()


def scores_of(alive, norms, table, vectors):
    blocks = alive.shape[0]
    rows, width = vectors.shape
    lists = table.shape[0]
    return pl.pallas_call(
        scores_kernel,
        out_shape=shaped((rows, lists), F32),
        in_specs=[VMEM] * 4,
        out_specs=HBM,
        scratch_shapes=[pltpu.VMEM((rows, lists), F32), pltpu.SemaphoreType.DMA((blocks // 4,))],
        compiler_params=params(24),
        cost_estimate=cost(2 * lists * rows * width, 4 * rows * lists),
        name="scores",
    )(alive, norms, table, vectors)


def merge_kernel(picks_ref, alive_ref, *refs):
    steps = picks_ref.shape[0]
    parts, out_ref, held, sems = refs[:steps], refs[steps + 1], refs[steps + 2], refs[steps + 3]
    block, lists = parts[0].shape

    def store(k):
        start = pl.multiple_of(picks_ref[k] * block, block)
        return pltpu.make_async_copy(held.at[k], out_ref.at[pl.ds(start, block), :], sems.at[k])

    for k in range(steps):

        @pl.when(picks_ref[k] >= 0)
        def _():
            weights = turned_weights(alive_ref[pl.ds(picks_ref[k], 1), :])
            weights = jnp.concatenate([weights] * (lists // 128), axis=1)
            held[k] = parts[k][...].astype(F32) * weights
            store(k).start()

    for k in range(steps):

        @pl.when(picks_ref[k] >= 0)
        def _():
            store(k).wait()


def merge(picks, alive, parts, scores):
    steps = len(parts)
    block, lists = parts[0].shape
    return pl.pallas_call(
        merge_kernel,
        out_shape=shaped(scores.shape, scores.dtype),
        in_specs=[SMEM, VMEM] + [VMEM] * steps + [HBM],
        out_specs=HBM,
        scratch_shapes=[pltpu.VMEM((steps, block, lists), F32), pltpu.SemaphoreType.DMA((steps,))],
        input_output_aliases={2 + steps: 0},
        compiler_params=params(8),
        cost_estimate=cost(2 * steps * block * lists, 6 * steps * block * lists),
        name="merge",
    )(picks, alive, *parts, scores)


def local(vectors, keep_bits, counts, block_list, home_pos, old_centroids):
    n_groups = lax.axis_size("grp")
    n_rows = lax.axis_size("row")
    blocks = counts.shape[0]
    block = vectors.shape[0] // blocks
    lists_group = old_centroids.shape[0]
    keep = keep_bits.reshape(blocks, block)
    there = [[(i, peer(i, k, n_groups)) for i in range(n_groups)] for k in range(1, n_groups)]
    back = [[(j, i) for i, j in pairs] for pairs in there]
    chips = n_rows // 2
    along = [[(i, 2 * peer(i // 2, k, chips) + i % 2) for i in range(n_rows)] for k in range(1, chips)]
    cores = [(i, i ^ 1) for i in range(n_rows)]

    alive, meta, picks, heads, rows = movers(n_groups, lists_group, block_list, home_pos, counts, keep, vectors)
    heads = [lax.ppermute(x, "grp", pairs) for x, pairs in zip(heads, there)]
    sums = block_sums(alive, vectors)
    last, sums, *heads = lax.optimization_barrier((rows[-1], sums, *heads))
    last = lax.ppermute(last, "grp", there[-1])
    mine = pack(meta, sums, heads)
    mine, *rows = lax.optimization_barrier((mine, *rows[:-1]))
    rows = [lax.ppermute(x, "grp", pairs) for x, pairs in zip(rows, there)]
    near = [lax.ppermute(mine, "row", pairs) for pairs in along]
    sums, totals = with_prior(blocks, mine, old_centroids)
    both = jnp.concatenate([mine] + near, axis=0)
    both, last = lax.optimization_barrier((both, last))
    rows.append(last)
    far = lax.ppermute(both, "row", cores)
    table, norms, share = make_table(n_rows, blocks, near, far, sums, totals)
    parts = parts_of(norms, table, rows)
    parts = [lax.ppermute(x, "grp", pairs) for x, pairs in zip(parts, back)]
    scores = scores_of(alive, norms, table, vectors)
    scores = merge(picks, alive, parts, scores)
    return (share, scores)


def solution(mesh):
    in_specs = (
        P(("grp", "row"), None),
        P(("grp", "row")),
        P(("grp", "row")),
        P(),
        P(),
        P("grp", None),
    )
    out_specs = (P(("grp", "row"), None), P(("grp", "row"), None))
    return jax.shard_map(local, mesh=mesh, in_specs=in_specs, out_specs=out_specs, check_vma=False)
```

```python
import functools
import math

import jax
import jax.numpy as jnp
from jax import lax
from jax.experimental import pallas as pl
from jax.experimental.pallas import tpu as pltpu
from jax.sharding import PartitionSpec as P

PRIOR = 16
MIB = 1 << 20
F32 = jnp.float32
BF16 = jnp.bfloat16
I16 = jnp.int16
I32 = jnp.int32
ROW_DIMS = (((1,), (1,)), ((), ()))
COL_DIMS = (((0,), (0,)), ((), ()))
VMEM = pl.BlockSpec(memory_space=pltpu.VMEM)
SMEM = pl.BlockSpec(memory_space=pltpu.SMEM)
HBM = pl.BlockSpec(memory_space=pltpu.HBM)


def peer(index, step, size):
    if size & (size - 1) == 0:
        return index ^ step
    return (index + step) % size


def power(exponent):
    return jnp.exp2(exponent).astype(BF16).astype(F32)


def iota(shape, dim):
    return lax.broadcasted_iota(I32, shape, dim)


def shaped(shape, dtype):
    return jax.ShapeDtypeStruct(shape, dtype)


def params(mib):
    return pltpu.CompilerParams(vmem_limit_bytes=mib * MIB)


def cost(flops, size):
    return pl.CostEstimate(flops=flops, bytes_accessed=size, transcendentals=0)


def in_hbm(array):
    return pltpu.with_memory_space_constraint(array, pltpu.HBM)


def as_lanes(column):
    rows = column.shape[0]
    wide = jnp.broadcast_to(column, (rows, 128))
    return jnp.transpose(jnp.concatenate([wide, jnp.zeros((128 - rows, 128), F32)], axis=0))[0:1, :]


def coded_rows(values):
    largest = jnp.maximum(jnp.max(jnp.abs(values), axis=1, keepdims=True), 2.0**-80)
    exponent = jnp.ceil(jnp.log2(largest) + 0.001) - 15.0
    return jnp.round(values * power(-exponent)).astype(I32), exponent


def turned_weights(weights):
    return jnp.transpose(jnp.broadcast_to(weights, (128, 128)))


def movers_kernel(n_groups, lists_group, list_ref, pos_ref, counts_ref, keep_ref, vec_ref, *refs):
    steps = n_groups - 1
    alive_ref, meta_ref, picks_ref = refs[:3]
    head_refs, row_refs = refs[3 : 3 + steps], refs[3 + steps : 3 + 2 * steps]
    lists, pos, fill, held, sems = refs[3 + 2 * steps :]
    loads = [
        pltpu.make_async_copy(src, dst, sems.at[steps + i])
        for i, (src, dst) in enumerate([(list_ref, lists), (pos_ref, pos), (counts_ref, fill), (keep_ref, held)])
    ]
    for load in loads:
        load.start()
    blocks, block = keep_ref.shape
    group = lax.axis_index("grp")
    base = (group * lax.axis_size("row") + lax.axis_index("row")) * blocks
    lane = iota((1, block), 1)
    row = iota((blocks, block), 0)
    slots = jnp.full((1, block), -1, I32)
    filled = jnp.zeros((blocks, block), I32)
    picks = [jnp.int32(-1)] * steps
    homes = [jnp.int32(-1)] * steps
    for load in loads:
        load.wait()
    for b in range(blocks):
        home = pos[lists[base + b]]
        home_group = home // lists_group
        slot = home - home_group * lists_group
        slots = jnp.where((lane == b) & (home_group == group), slot, slots)
        for k in range(steps):
            hit = home_group == peer(group, k + 1, n_groups)
            picks[k] = jnp.where(hit, b, picks[k])
            homes[k] = jnp.where(hit, slot, homes[k])
    fetches = []
    for k in range(steps):
        picks_ref[k] = picks[k]
        start = pl.multiple_of(jnp.maximum(picks[k], 0) * block, block)
        fetches.append(pltpu.make_async_copy(vec_ref.at[pl.ds(start, block), :], row_refs[k], sems.at[k]))
        fetches[k].start()
    for b in range(blocks):
        filled = jnp.where(row == b, fill[b], filled)
    alive = held[...].astype(F32) * (iota((blocks, block), 1) < filled).astype(F32)
    alive_ref[...] = alive
    ones = jnp.ones((8, block), BF16)
    block_counts = lax.dot_general(ones, alive.astype(BF16), ROW_DIMS, preferred_element_type=F32)
    meta_ref[...] = jnp.zeros_like(meta_ref)
    meta_ref[0:1, :] = slots.astype(F32)
    meta_ref[1:2, 0:blocks] = block_counts[0:1, :]
    for k in range(steps):
        fetches[k].wait()
        weights = alive_ref[pl.ds(jnp.maximum(picks[k], 0), 1), :]
        wide = jnp.broadcast_to(weights, (16, block)).astype(BF16)
        total = jnp.dot(wide, row_refs[k][...], preferred_element_type=F32)
        chunks = total.shape[1] // 128
        for j in range(chunks):
            head_refs[k][j : j + 1, :] = total[0:1, j * 128 : (j + 1) * 128]
        head_refs[k][chunks : chunks + 8, :] = jnp.concatenate(
            [
                jnp.broadcast_to(jnp.sum(weights, axis=1, keepdims=True), (1, 128)),
                jnp.broadcast_to(homes[k].astype(F32), (1, 128)),
                jnp.zeros((6, 128), F32),
            ],
            axis=0,
        )


def movers(n_groups, lists_group, block_list, home_pos, counts, keep, vectors):
    steps = n_groups - 1
    blocks, block = keep.shape
    width = vectors.shape[1]
    outs = pl.pallas_call(
        functools.partial(movers_kernel, n_groups, lists_group),
        out_shape=[shaped((blocks, block), F32), shaped((8, block), F32), shaped((steps,), I32)]
        + [shaped((width // 128 + 8, 128), F32)] * steps
        + [shaped((block, width), BF16)] * steps,
        in_specs=[HBM] * 5,
        out_specs=[VMEM, VMEM, SMEM] + [VMEM] * (2 * steps),
        scratch_shapes=[
            pltpu.SMEM(block_list.shape, I32),
            pltpu.SMEM(home_pos.shape, I32),
            pltpu.SMEM(counts.shape, I32),
            pltpu.VMEM(keep.shape, I32),
            pltpu.SemaphoreType.DMA((steps + 4,)),
        ],
        compiler_params=params(8),
        cost_estimate=cost(2 * steps * block * width, 6 * steps * block * width),
        name="movers",
    )(*map(in_hbm, (block_list, home_pos, counts, keep, vectors)))
    return outs[0], outs[1], outs[2], outs[3 : 3 + steps], outs[3 + steps :]


def sums_kernel(alive_ref, vec_ref, sums_ref):
    blocks, block = alive_ref.shape
    tile = 8
    row = iota((tile, block), 0)
    for t in range(blocks // tile):
        alive = alive_ref[t * tile : (t + 1) * tile, :]
        spread = jnp.concatenate([jnp.where(row == j, alive, 0.0) for j in range(tile)], axis=1)
        rows = vec_ref[t * tile * block : (t + 1) * tile * block, :]
        sums_ref[t * tile : (t + 1) * tile, :] = jnp.dot(spread.astype(BF16), rows, preferred_element_type=F32)


def block_sums(alive, vectors):
    blocks = alive.shape[0]
    rows, width = vectors.shape
    return pl.pallas_call(
        sums_kernel,
        out_shape=shaped((blocks, width), F32),
        in_specs=[VMEM] * 2,
        out_specs=VMEM,
        compiler_params=params(16),
        cost_estimate=cost(16 * rows * width, 2 * rows * width),
        name="block_sums",
    )(alive, vectors)


def pack_kernel(meta_ref, sums_ref, *refs):
    heads, out_ref = refs[:-1], refs[-1]
    blocks, width = sums_ref.shape
    rows = out_ref.shape[0]
    chunks = width // 128
    lane = iota((1, 128), 1)
    slots, counts = meta_ref[0:1, :], meta_ref[1:2, :]
    arrived = []
    for k, head in enumerate(heads):
        arrived.append(jnp.concatenate([head[j : j + 1, :] for j in range(chunks)], axis=1))
        slots = jnp.where(lane == blocks + k, head[chunks + 1 : chunks + 2, :], slots)
        counts = jnp.where(lane == blocks + k, head[chunks : chunks + 1, :], counts)
    spare = rows - blocks - len(heads)
    coded, exponent = coded_rows(
        jnp.concatenate([sums_ref[...]] + arrived + [jnp.zeros((spare, width), F32)], axis=0)
    )
    extra = jnp.concatenate([slots, counts, as_lanes(exponent)], axis=0).astype(I32)
    extra = jnp.concatenate([extra, jnp.zeros((3, width - 128), I32)], axis=1)
    out_ref[...] = jnp.concatenate([coded[: rows - 3], extra], axis=0).astype(I16)


def pack(meta, sums, heads):
    blocks, width = sums.shape
    rows = blocks + -(-(len(heads) + 3) // 8) * 8
    return pl.pallas_call(
        pack_kernel,
        out_shape=shaped((rows, width), I16),
        in_specs=[VMEM] * (2 + len(heads)),
        out_specs=VMEM,
        compiler_params=params(8),
        cost_estimate=cost(6 * 10**9, 6 * rows * width),
        name="pack",
    )(meta, sums, *heads)


def add_up(sources, blocks, lists):
    rows, width = sources[0].shape
    span = 4 if rows - blocks == 8 else rows - blocks
    fill = -len(sources) % (8 // span) if span < 8 else 0
    big = jnp.concatenate([x[:blocks] for x in sources], axis=0)
    small = [x[blocks : blocks + span] for x in sources] + [jnp.zeros((span, width), I32)] * fill
    small = jnp.concatenate(small, axis=0)

    def lanes(which, spare):
        facts = [x[rows - 3 + which : rows - 2 + which, 0:128].astype(F32) for x in sources]
        wide = jnp.concatenate([x[:, 0:blocks] for x in facts], axis=1)
        tail = [x[:, blocks : blocks + span] for x in facts] + [jnp.full((1, span), spare, F32)] * fill
        return wide, jnp.concatenate(tail, axis=1)

    def four(pair, low=True):
        wide, tail = pair
        return jnp.concatenate([wide, wide * low, tail, tail * low], axis=1)

    slots = four(lanes(0, -1.0))
    counts = four(lanes(1, 0.0), low=False)
    scale, scale_small = map(power, lanes(2, 0.0))
    scale = jnp.concatenate([256.0 * scale, scale, 256.0 * scale_small, scale_small], axis=1)
    hit = iota((lists, slots.shape[1]), 0) == slots.astype(I32)
    totals = jnp.sum(jnp.where(hit, counts, 0.0), axis=1, keepdims=True)
    values = jnp.concatenate([big >> 8, big & 255, small >> 8, small & 255], axis=0)
    sums = jnp.dot(
        jnp.where(hit, scale, 0.0).astype(BF16), values.astype(F32).astype(BF16), preferred_element_type=F32
    )
    return sums, totals


def prior_kernel(blocks, mine_ref, old_ref, sums_ref, totals_ref):
    lists = old_ref.shape[0]
    prior = 1.0 * PRIOR
    sums, totals = add_up([mine_ref[...].astype(I32)], blocks, lists)
    sums_ref[...] = sums + prior * old_ref[...].astype(F32)
    totals_ref[...] = jnp.broadcast_to(totals + prior, totals_ref.shape)


def with_prior(blocks, mine, old):
    lists, width = old.shape
    return pl.pallas_call(
        functools.partial(prior_kernel, blocks),
        out_shape=[shaped((lists, width), F32), shaped((lists, 128), F32)],
        in_specs=[VMEM] * 2,
        out_specs=[VMEM] * 2,
        compiler_params=params(16),
        cost_estimate=cost(20000 * lists * width, 8 * lists * width),
        name="prior",
    )(mine, old)


def table_kernel(blocks, n_near, *refs):
    near, far = refs[:n_near], refs[n_near]
    sums_ref, totals_ref, table_ref, norms_ref, share_ref = refs[n_near + 1 :]
    lists, width = sums_ref.shape
    rows = near[0].shape[0]
    sources = [ref[...].astype(I32) for ref in near]
    sources += [far[j * rows : (j + 1) * rows, :].astype(I32) for j in range(n_near + 1)]
    sums, totals = add_up(sources, blocks, lists)
    totals = totals_ref[:, 0:1] + totals
    table = ((sums_ref[...] + sums) * (1.0 / totals)).astype(BF16)
    table_ref[...] = table
    share = share_ref.shape[0]
    start = pl.multiple_of(lax.axis_index("row") * share, share)
    share_ref[...] = table_ref[pl.ds(start, share), :]
    squares = jnp.square(table.astype(F32))
    partial = squares[:, 0:128]
    for j in range(1, width // 128):
        partial = partial + squares[:, j * 128 : (j + 1) * 128]
    ones = jnp.ones((16, 128), BF16)
    norms = jnp.zeros((16, lists), F32)
    for _ in range(3):
        piece = partial.astype(BF16)
        partial = partial - piece.astype(F32)
        norms = norms + lax.dot_general(ones, piece, ROW_DIMS, preferred_element_type=F32)
    norms_ref[...] = norms[0:8] * (1.0 / math.sqrt(width))


def make_table(n_rows, blocks, near, far, sums, totals):
    lists, width = sums.shape
    return pl.pallas_call(
        functools.partial(table_kernel, blocks, len(near)),
        out_shape=[shaped((lists, width), BF16), shaped((8, lists), F32), shaped((lists // n_rows, width), BF16)],
        in_specs=[VMEM] * (len(near) + 3),
        out_specs=[VMEM] * 3,
        compiler_params=params(24),
        cost_estimate=cost(2000 * lists * width, 8 * lists * width),
        name="table",
    )(*near, far, sums, totals)


def parts_kernel(norms_ref, table_ref, *refs):
    steps = len(refs) // 2
    factor = 1.0 / math.sqrt(table_ref.shape[1])
    norms = norms_ref[0:1, :]
    for row_ref, part_ref in zip(refs[:steps], refs[steps:]):
        dots = lax.dot_general(row_ref[...], table_ref[...], ROW_DIMS, preferred_element_type=F32)
        part_ref[...] = (dots * (2.0 * factor) - norms).astype(part_ref.dtype)


def parts_of(norms, table, rows):
    lists, width = table.shape
    block = rows[0].shape[0]
    return pl.pallas_call(
        parts_kernel,
        out_shape=[shaped((block, lists), BF16)] * len(rows),
        in_specs=[VMEM] * (2 + len(rows)),
        out_specs=[VMEM] * len(rows),
        compiler_params=params(16),
        cost_estimate=cost(2 * len(rows) * block * lists * width, 2 * lists * width),
        name="parts",
    )(norms, table, *rows)


def scores_kernel(alive_ref, norms_ref, table_ref, vec_ref, out_ref, held, sems):
    blocks, block = alive_ref.shape
    lists, width = table_ref.shape
    factor = 1.0 / math.sqrt(width)
    norms = norms_ref[0:1, :]
    table = table_ref[...]
    tile = 4
    stores = []
    for t in range(blocks // tile):
        span = slice(t * tile * block, (t + 1) * tile * block)
        dots = lax.dot_general(vec_ref[span, :], table, ROW_DIMS, preferred_element_type=F32)
        for j in range(tile):
            b = t * tile + j
            weights = jnp.concatenate([turned_weights(alive_ref[b : b + 1, :])] * (lists // 128), axis=1)
            part = dots[j * block : (j + 1) * block, :]
            held[b * block : (b + 1) * block, :] = (part * (2.0 * factor) - norms) * weights
        stores.append(pltpu.make_async_copy(held.at[span, :], out_ref.at[span, :], sems.at[t]))
        stores[t].start()
    for store in stores:
        store.wait()


def scores_of(alive, norms, table, vectors):
    blocks = alive.shape[0]
    rows, width = vectors.shape
    lists = table.shape[0]
    return pl.pallas_call(
        scores_kernel,
        out_shape=shaped((rows, lists), F32),
        in_specs=[VMEM] * 4,
        out_specs=HBM,
        scratch_shapes=[pltpu.VMEM((rows, lists), F32), pltpu.SemaphoreType.DMA((blocks // 4,))],
        compiler_params=params(24),
        cost_estimate=cost(2 * lists * rows * width, 4 * rows * lists),
        name="scores",
    )(alive, norms, table, vectors)


def merge_kernel(picks_ref, alive_ref, *refs):
    steps = picks_ref.shape[0]
    parts, out_ref, held, sems = refs[:steps], refs[steps + 1], refs[steps + 2], refs[steps + 3]
    block, lists = parts[0].shape

    def store(k):
        start = pl.multiple_of(picks_ref[k] * block, block)
        return pltpu.make_async_copy(held.at[k], out_ref.at[pl.ds(start, block), :], sems.at[k])

    for k in range(steps):

        @pl.when(picks_ref[k] >= 0)
        def _():
            weights = turned_weights(alive_ref[pl.ds(picks_ref[k], 1), :])
            weights = jnp.concatenate([weights] * (lists // 128), axis=1)
            held[k] = parts[k][...].astype(F32) * weights
            store(k).start()

    for k in range(steps):

        @pl.when(picks_ref[k] >= 0)
        def _():
            store(k).wait()


def merge(picks, alive, parts, scores):
    steps = len(parts)
    block, lists = parts[0].shape
    return pl.pallas_call(
        merge_kernel,
        out_shape=shaped(scores.shape, scores.dtype),
        in_specs=[SMEM, VMEM] + [VMEM] * steps + [HBM],
        out_specs=HBM,
        scratch_shapes=[pltpu.VMEM((steps, block, lists), F32), pltpu.SemaphoreType.DMA((steps,))],
        input_output_aliases={2 + steps: 0},
        compiler_params=params(8),
        cost_estimate=cost(2 * steps * block * lists, 6 * steps * block * lists),
        name="merge",
    )(picks, alive, *parts, scores)


def local(vectors, keep_bits, counts, block_list, home_pos, old_centroids):
    n_groups = lax.axis_size("grp")
    n_rows = lax.axis_size("row")
    blocks = counts.shape[0]
    block = vectors.shape[0] // blocks
    lists_group = old_centroids.shape[0]
    keep = keep_bits.reshape(blocks, block)
    there = [[(i, peer(i, k, n_groups)) for i in range(n_groups)] for k in range(1, n_groups)]
    back = [[(j, i) for i, j in pairs] for pairs in there]
    chips = n_rows // 2
    along = [[(i, 2 * peer(i // 2, k, chips) + i % 2) for i in range(n_rows)] for k in range(1, chips)]
    cores = [(i, i ^ 1) for i in range(n_rows)]

    alive, meta, picks, heads, rows = movers(n_groups, lists_group, block_list, home_pos, counts, keep, vectors)
    heads = [lax.ppermute(x, "grp", pairs) for x, pairs in zip(heads, there)]
    sums = block_sums(alive, vectors)
    last = lax.ppermute(rows[-1], "grp", there[-1])
    mine = pack(meta, sums, heads)
    mine, *rows = lax.optimization_barrier((mine, *rows[:-1]))
    rows = [lax.ppermute(x, "grp", pairs) for x, pairs in zip(rows, there)]
    near = [lax.ppermute(mine, "row", pairs) for pairs in along]
    sums, totals = with_prior(blocks, mine, old_centroids)
    both = jnp.concatenate([mine] + near, axis=0)
    both, last = lax.optimization_barrier((both, last))
    rows.append(last)
    far = lax.ppermute(both, "row", cores)
    table, norms, share = make_table(n_rows, blocks, near, far, sums, totals)
    parts = parts_of(norms, table, rows)
    parts = [lax.ppermute(x, "grp", pairs) for x, pairs in zip(parts, back)]
    scores = scores_of(alive, norms, table, vectors)
    scores = merge(picks, alive, parts, scores)
    return (share, scores)


def solution(mesh):
    in_specs = (
        P(("grp", "row"), None),
        P(("grp", "row")),
        P(("grp", "row")),
        P(),
        P(),
        P("grp", None),
    )
    out_specs = (P(("grp", "row"), None), P(("grp", "row"), None))
    return jax.shard_map(local, mesh=mesh, in_specs=in_specs, out_specs=out_specs, check_vma=False)
```

```python
import functools
import math

import jax
import jax.numpy as jnp
from jax import lax
from jax.experimental import pallas as pl
from jax.experimental.pallas import tpu as pltpu
from jax.sharding import PartitionSpec as P

PRIOR = 16
TAIL = 4
MIB = 1 << 20
F32 = jnp.float32
BF16 = jnp.bfloat16
I16 = jnp.int16
I32 = jnp.int32
ROW_DIMS = (((1,), (1,)), ((), ()))
COL_DIMS = (((0,), (0,)), ((), ()))
VMEM = pl.BlockSpec(memory_space=pltpu.VMEM)
SMEM = pl.BlockSpec(memory_space=pltpu.SMEM)
HBM = pl.BlockSpec(memory_space=pltpu.HBM)


def peer(index, step, size):
    if size & (size - 1) == 0:
        return index ^ step
    return (index + step) % size


def power(exponent):
    return jnp.exp2(exponent).astype(BF16).astype(F32)


def iota(shape, dim):
    return lax.broadcasted_iota(I32, shape, dim)


def shaped(shape, dtype):
    return jax.ShapeDtypeStruct(shape, dtype)


def params(mib):
    return pltpu.CompilerParams(vmem_limit_bytes=mib * MIB)


def cost(flops, size):
    return pl.CostEstimate(flops=flops, bytes_accessed=size, transcendentals=0)


def in_hbm(array):
    return pltpu.with_memory_space_constraint(array, pltpu.HBM)


def as_lanes(column):
    rows = column.shape[0]
    wide = jnp.broadcast_to(column, (rows, 128))
    return jnp.transpose(jnp.concatenate([wide, jnp.zeros((128 - rows, 128), F32)], axis=0))[0:1, :]


def coded_rows(values):
    largest = jnp.maximum(jnp.max(jnp.abs(values), axis=1, keepdims=True), 2.0**-80)
    exponent = jnp.ceil(jnp.log2(largest) + 0.001) - 15.0
    return jnp.round(values * power(-exponent)).astype(I32), exponent


def turned_weights(weights):
    return jnp.transpose(jnp.broadcast_to(weights, (128, 128)))


def movers_kernel(n_groups, lists_group, list_ref, pos_ref, counts_ref, keep_ref, vec_ref, *refs):
    steps = n_groups - 1
    alive_ref, meta_ref, picks_ref = refs[:3]
    head_refs, row_refs = refs[3 : 3 + steps], refs[3 + steps : 3 + 2 * steps]
    lists, pos, fill, held, sems = refs[3 + 2 * steps :]
    loads = [
        pltpu.make_async_copy(src, dst, sems.at[steps + i])
        for i, (src, dst) in enumerate([(list_ref, lists), (pos_ref, pos), (counts_ref, fill), (keep_ref, held)])
    ]
    for load in loads:
        load.start()
    blocks, block = keep_ref.shape
    group = lax.axis_index("grp")
    base = (group * lax.axis_size("row") + lax.axis_index("row")) * blocks
    lane = iota((1, block), 1)
    row = iota((blocks, block), 0)
    slots = jnp.full((1, block), -1, I32)
    filled = jnp.zeros((blocks, block), I32)
    picks = [jnp.int32(-1)] * steps
    homes = [jnp.int32(-1)] * steps
    for load in loads:
        load.wait()
    for b in range(blocks):
        home = pos[lists[base + b]]
        home_group = home // lists_group
        slot = home - home_group * lists_group
        slots = jnp.where((lane == b) & (home_group == group), slot, slots)
        for k in range(steps):
            hit = home_group == peer(group, k + 1, n_groups)
            picks[k] = jnp.where(hit, b, picks[k])
            homes[k] = jnp.where(hit, slot, homes[k])
    fetches = []
    for k in range(steps):
        picks_ref[k] = picks[k]
        start = pl.multiple_of(jnp.maximum(picks[k], 0) * block, block)
        fetches.append(pltpu.make_async_copy(vec_ref.at[pl.ds(start, block), :], row_refs[k], sems.at[k]))
        fetches[k].start()
    for b in range(blocks):
        filled = jnp.where(row == b, fill[b], filled)
    alive = held[...].astype(F32) * (iota((blocks, block), 1) < filled).astype(F32)
    alive_ref[...] = alive
    ones = jnp.ones((8, block), BF16)
    block_counts = lax.dot_general(ones, alive.astype(BF16), ROW_DIMS, preferred_element_type=F32)
    meta_ref[...] = jnp.zeros_like(meta_ref)
    meta_ref[0:1, :] = slots.astype(F32)
    meta_ref[1:2, 0:blocks] = block_counts[0:1, :]
    for k in range(steps):
        fetches[k].wait()
        weights = alive_ref[pl.ds(jnp.maximum(picks[k], 0), 1), :]
        wide = jnp.broadcast_to(weights, (16, block)).astype(BF16)
        total = jnp.dot(wide, row_refs[k][...], preferred_element_type=F32)
        chunks = total.shape[1] // 128
        for j in range(chunks):
            head_refs[k][j : j + 1, :] = total[0:1, j * 128 : (j + 1) * 128]
        head_refs[k][chunks : chunks + 8, :] = jnp.concatenate(
            [
                jnp.broadcast_to(jnp.sum(weights, axis=1, keepdims=True), (1, 128)),
                jnp.broadcast_to(homes[k].astype(F32), (1, 128)),
                jnp.zeros((6, 128), F32),
            ],
            axis=0,
        )


def movers(n_groups, lists_group, block_list, home_pos, counts, keep, vectors):
    steps = n_groups - 1
    blocks, block = keep.shape
    width = vectors.shape[1]
    outs = pl.pallas_call(
        functools.partial(movers_kernel, n_groups, lists_group),
        out_shape=[shaped((blocks, block), F32), shaped((8, block), F32), shaped((steps,), I32)]
        + [shaped((width // 128 + 8, 128), F32)] * steps
        + [shaped((block, width), BF16)] * steps,
        in_specs=[HBM] * 5,
        out_specs=[VMEM, VMEM, SMEM] + [VMEM] * (2 * steps),
        scratch_shapes=[
            pltpu.SMEM(block_list.shape, I32),
            pltpu.SMEM(home_pos.shape, I32),
            pltpu.SMEM(counts.shape, I32),
            pltpu.VMEM(keep.shape, I32),
            pltpu.SemaphoreType.DMA((steps + 4,)),
        ],
        compiler_params=params(8),
        cost_estimate=cost(2 * steps * block * width, 6 * steps * block * width),
        name="movers",
    )(*map(in_hbm, (block_list, home_pos, counts, keep, vectors)))
    return outs[0], outs[1], outs[2], outs[3 : 3 + steps], outs[3 + steps :]


def sums_kernel(alive_ref, vec_ref, sums_ref):
    blocks, block = alive_ref.shape
    tile = 8
    row = iota((tile, block), 0)
    for t in range(blocks // tile):
        alive = alive_ref[t * tile : (t + 1) * tile, :]
        spread = jnp.concatenate([jnp.where(row == j, alive, 0.0) for j in range(tile)], axis=1)
        rows = vec_ref[t * tile * block : (t + 1) * tile * block, :]
        sums_ref[t * tile : (t + 1) * tile, :] = jnp.dot(spread.astype(BF16), rows, preferred_element_type=F32)


def block_sums(alive, vectors):
    blocks = alive.shape[0]
    rows, width = vectors.shape
    return pl.pallas_call(
        sums_kernel,
        out_shape=shaped((blocks, width), F32),
        in_specs=[VMEM] * 2,
        out_specs=VMEM,
        compiler_params=params(16),
        cost_estimate=cost(16 * rows * width, 2 * rows * width),
        name="block_sums",
    )(alive, vectors)


def pack_kernel(meta_ref, sums_ref, *refs):
    heads, out_ref = refs[:-1][::-1], refs[-1]
    blocks, width = sums_ref.shape
    chunks = width // 128
    lane = iota((1, 128), 1)
    slots, counts = meta_ref[0:1, :], meta_ref[1:2, :]
    arrived = []
    for k, head in enumerate(heads):
        arrived.append(jnp.concatenate([head[j : j + 1, :] for j in range(chunks)], axis=1))
        slots = jnp.where(lane == blocks + k, head[chunks + 1 : chunks + 2, :], slots)
        counts = jnp.where(lane == blocks + k, head[chunks : chunks + 1, :], counts)
    coded, exponent = coded_rows(jnp.concatenate([sums_ref[...]] + arrived, axis=0))
    facts = jnp.concatenate([slots, counts, as_lanes(exponent)], axis=1).astype(I32)
    facts = jnp.concatenate([facts, jnp.zeros((1, width - 384), I32)], axis=1)
    tail = jnp.concatenate([coded[blocks:]] + [jnp.zeros((1, width), I32)] * (TAIL - 1 - len(heads)) + [facts], axis=0)
    parts = [coded[j : j + 8] for j in range(0, blocks, 8)]
    parts.append(jnp.concatenate([tail[:, : width // 2], tail[:, width // 2 :]], axis=0))
    out_ref[...] = jnp.concatenate(parts, axis=1).astype(I16)


def pack(meta, sums, heads):
    blocks, width = sums.shape
    size = blocks // 8 * width + width // 2
    return pl.pallas_call(
        pack_kernel,
        out_shape=shaped((8, size), I16),
        in_specs=[VMEM] * (2 + len(heads)),
        out_specs=VMEM,
        compiler_params=params(8),
        cost_estimate=cost(6 * 10**9, 48 * size),
        name="pack",
    )(meta, sums, *heads[::-1])


def unpacked(packed, blocks, width):
    big = jnp.concatenate([packed[:, j * width : (j + 1) * width] for j in range(blocks // 8)], axis=0)
    tail = packed[:, blocks // 8 * width :]
    return big, jnp.concatenate([tail[:TAIL], tail[TAIL:]], axis=1)


def add_up(sources, blocks, lists, width):
    sources = [unpacked(x, blocks, width) for x in sources]
    fill = len(sources) % 2
    big = jnp.concatenate([x for x, _ in sources], axis=0)
    small = jnp.concatenate([x for _, x in sources] + [jnp.zeros((TAIL, width), I32)] * fill, axis=0)

    def lanes(which, spare):
        facts = [x[TAIL - 1 :, 128 * which : 128 * which + 128].astype(F32) for _, x in sources]
        wide = jnp.concatenate([x[:, 0:blocks] for x in facts], axis=1)
        tail = [x[:, blocks : blocks + TAIL] for x in facts] + [jnp.full((1, TAIL), spare, F32)] * fill
        return wide, jnp.concatenate(tail, axis=1)

    def four(pair, low=True):
        wide, tail = pair
        return jnp.concatenate([wide, wide * low, tail, tail * low], axis=1)

    slots = four(lanes(0, -1.0))
    counts = four(lanes(1, 0.0), low=False)
    scale, scale_small = map(power, lanes(2, 0.0))
    scale = jnp.concatenate([256.0 * scale, scale, 256.0 * scale_small, scale_small], axis=1)
    hit = iota((lists, slots.shape[1]), 0) == slots.astype(I32)
    totals = jnp.sum(jnp.where(hit, counts, 0.0), axis=1, keepdims=True)
    values = jnp.concatenate([big >> 8, big & 255, small >> 8, small & 255], axis=0)
    sums = jnp.dot(
        jnp.where(hit, scale, 0.0).astype(BF16), values.astype(F32).astype(BF16), preferred_element_type=F32
    )
    return sums, totals


def prior_kernel(blocks, mine_ref, old_ref, sums_ref, totals_ref):
    lists = old_ref.shape[0]
    prior = 1.0 * PRIOR
    sums, totals = add_up([mine_ref[...].astype(I32)], blocks, lists, old_ref.shape[1])
    sums_ref[...] = sums + prior * old_ref[...].astype(F32)
    totals_ref[...] = jnp.broadcast_to(totals + prior, totals_ref.shape)


def with_prior(blocks, mine, old):
    lists, width = old.shape
    return pl.pallas_call(
        functools.partial(prior_kernel, blocks),
        out_shape=[shaped((lists, width), F32), shaped((lists, 128), F32)],
        in_specs=[VMEM] * 2,
        out_specs=[VMEM] * 2,
        compiler_params=params(16),
        cost_estimate=cost(20000 * lists * width, 8 * lists * width),
        name="prior",
    )(mine, old)


def table_kernel(blocks, n_near, *refs):
    near, far = refs[:n_near], refs[n_near]
    sums_ref, totals_ref, table_ref, norms_ref, share_ref = refs[n_near + 1 :]
    lists, width = sums_ref.shape
    rows = near[0].shape[0]
    sources = [ref[...].astype(I32) for ref in near]
    far_all = far[...].astype(I32)
    sources += [far_all[j * rows : (j + 1) * rows] for j in range(n_near + 1)]
    sums, totals = add_up(sources, blocks, lists, width)
    totals = totals_ref[:, 0:1] + totals
    table = ((sums_ref[...] + sums) * (1.0 / totals)).astype(BF16)
    table_ref[...] = table
    share = share_ref.shape[0]
    start = pl.multiple_of(lax.axis_index("row") * share, share)
    share_ref[...] = table_ref[pl.ds(start, share), :]
    squares = jnp.square(table.astype(F32))
    partial = squares[:, 0:128]
    for j in range(1, width // 128):
        partial = partial + squares[:, j * 128 : (j + 1) * 128]
    ones = jnp.ones((16, 128), BF16)
    norms = jnp.zeros((16, lists), F32)
    for _ in range(3):
        piece = partial.astype(BF16)
        partial = partial - piece.astype(F32)
        norms = norms + lax.dot_general(ones, piece, ROW_DIMS, preferred_element_type=F32)
    norms_ref[...] = norms[0:8] * (1.0 / math.sqrt(width))


def make_table(n_rows, blocks, near, far, sums, totals):
    lists, width = sums.shape
    return pl.pallas_call(
        functools.partial(table_kernel, blocks, len(near)),
        out_shape=[shaped((lists, width), BF16), shaped((8, lists), F32), shaped((lists // n_rows, width), BF16)],
        in_specs=[VMEM] * (len(near) + 3),
        out_specs=[VMEM] * 3,
        compiler_params=params(24),
        cost_estimate=cost(2000 * lists * width, 8 * lists * width),
        name="table",
    )(*near, far, sums, totals)


def parts_kernel(norms_ref, table_ref, *refs):
    steps = len(refs) // 2
    factor = 1.0 / math.sqrt(table_ref.shape[1])
    norms = norms_ref[0:1, :]
    for row_ref, part_ref in zip(refs[:steps], refs[steps:]):
        dots = lax.dot_general(row_ref[...], table_ref[...], ROW_DIMS, preferred_element_type=F32)
        part_ref[...] = (dots * (2.0 * factor) - norms).astype(part_ref.dtype)


def parts_of(norms, table, rows):
    lists, width = table.shape
    block = rows[0].shape[0]
    return pl.pallas_call(
        parts_kernel,
        out_shape=[shaped((block, lists), BF16)] * len(rows),
        in_specs=[VMEM] * (2 + len(rows)),
        out_specs=[VMEM] * len(rows),
        compiler_params=params(16),
        cost_estimate=cost(2 * len(rows) * block * lists * width, 2 * lists * width),
        name="parts",
    )(norms, table, *rows)


def scores_kernel(alive_ref, norms_ref, table_ref, vec_ref, out_ref, held, sems):
    blocks, block = alive_ref.shape
    lists, width = table_ref.shape
    factor = 1.0 / math.sqrt(width)
    norms = norms_ref[0:1, :]
    table = table_ref[...]
    tile = 4
    stores = []
    for t in range(blocks // tile):
        span = slice(t * tile * block, (t + 1) * tile * block)
        dots = lax.dot_general(vec_ref[span, :], table, ROW_DIMS, preferred_element_type=F32)
        for j in range(tile):
            b = t * tile + j
            weights = jnp.concatenate([turned_weights(alive_ref[b : b + 1, :])] * (lists // 128), axis=1)
            part = dots[j * block : (j + 1) * block, :]
            held[b * block : (b + 1) * block, :] = (part * (2.0 * factor) - norms) * weights
        stores.append(pltpu.make_async_copy(held.at[span, :], out_ref.at[span, :], sems.at[t]))
        stores[t].start()
    for store in stores:
        store.wait()


def scores_of(alive, norms, table, vectors):
    blocks = alive.shape[0]
    rows, width = vectors.shape
    lists = table.shape[0]
    return pl.pallas_call(
        scores_kernel,
        out_shape=shaped((rows, lists), F32),
        in_specs=[VMEM] * 4,
        out_specs=HBM,
        scratch_shapes=[pltpu.VMEM((rows, lists), F32), pltpu.SemaphoreType.DMA((blocks // 4,))],
        compiler_params=params(24),
        cost_estimate=cost(2 * lists * rows * width, 4 * rows * lists),
        name="scores",
    )(alive, norms, table, vectors)


def merge_kernel(picks_ref, alive_ref, *refs):
    steps = picks_ref.shape[0]
    parts, out_ref, held, sems = refs[:steps], refs[steps + 1], refs[steps + 2], refs[steps + 3]
    block, lists = parts[0].shape

    def store(k):
        start = pl.multiple_of(picks_ref[k] * block, block)
        return pltpu.make_async_copy(held.at[k], out_ref.at[pl.ds(start, block), :], sems.at[k])

    for k in range(steps):

        @pl.when(picks_ref[k] >= 0)
        def _():
            weights = turned_weights(alive_ref[pl.ds(picks_ref[k], 1), :])
            weights = jnp.concatenate([weights] * (lists // 128), axis=1)
            held[k] = parts[k][...].astype(F32) * weights
            store(k).start()

    for k in range(steps):

        @pl.when(picks_ref[k] >= 0)
        def _():
            store(k).wait()


def merge(picks, alive, parts, scores):
    steps = len(parts)
    block, lists = parts[0].shape
    return pl.pallas_call(
        merge_kernel,
        out_shape=shaped(scores.shape, scores.dtype),
        in_specs=[SMEM, VMEM] + [VMEM] * steps + [HBM],
        out_specs=HBM,
        scratch_shapes=[pltpu.VMEM((steps, block, lists), F32), pltpu.SemaphoreType.DMA((steps,))],
        input_output_aliases={2 + steps: 0},
        compiler_params=params(8),
        cost_estimate=cost(2 * steps * block * lists, 6 * steps * block * lists),
        name="merge",
    )(picks, alive, *parts, scores)


def local(vectors, keep_bits, counts, block_list, home_pos, old_centroids):
    n_groups = lax.axis_size("grp")
    n_rows = lax.axis_size("row")
    blocks = counts.shape[0]
    block = vectors.shape[0] // blocks
    lists_group = old_centroids.shape[0]
    keep = keep_bits.reshape(blocks, block)
    there = [[(i, peer(i, k, n_groups)) for i in range(n_groups)] for k in range(1, n_groups)]
    back = [[(j, i) for i, j in pairs] for pairs in there]
    chips = n_rows // 2
    along = [[(i, 2 * peer(i // 2, k, chips) + i % 2) for i in range(n_rows)] for k in range(1, chips)]
    cores = [(i, i ^ 1) for i in range(n_rows)]

    alive, meta, picks, heads, rows = movers(n_groups, lists_group, block_list, home_pos, counts, keep, vectors)
    heads = [lax.ppermute(x, "grp", pairs) for x, pairs in zip(heads[::-1], there[::-1])][::-1]
    sums = block_sums(alive, vectors)
    last = lax.ppermute(rows[-1], "grp", there[-1])
    mine = pack(meta, sums, heads)
    mine, *rows = lax.optimization_barrier((mine, *rows[:-1]))
    rows = [lax.ppermute(x, "grp", pairs) for x, pairs in zip(rows, there)]
    near = [lax.ppermute(mine, "row", pairs) for pairs in along]
    sums, totals = with_prior(blocks, mine, old_centroids)
    near, last = lax.optimization_barrier((near, last))
    both = jnp.concatenate([mine] + near, axis=0)
    rows.append(last)
    far = lax.ppermute(both, "row", cores)
    table, norms, share = make_table(n_rows, blocks, near, far, sums, totals)
    parts = parts_of(norms, table, rows)
    parts = [lax.ppermute(x, "grp", pairs) for x, pairs in zip(parts, back)]
    scores = scores_of(alive, norms, table, vectors)
    scores = merge(picks, alive, parts, scores)
    return (share, scores)


def solution(mesh):
    in_specs = (
        P(("grp", "row"), None),
        P(("grp", "row")),
        P(("grp", "row")),
        P(),
        P(),
        P("grp", None),
    )
    out_specs = (P(("grp", "row"), None), P(("grp", "row"), None))
    return jax.shard_map(local, mesh=mesh, in_specs=in_specs, out_specs=out_specs, check_vma=False)
```

```python
import functools
import math

import jax
import jax.numpy as jnp
from jax import lax
from jax.experimental import pallas as pl
from jax.experimental.pallas import tpu as pltpu
from jax.sharding import PartitionSpec as P

PRIOR = 16
TAIL = 4
MIB = 1 << 20
F32 = jnp.float32
BF16 = jnp.bfloat16
I16 = jnp.int16
I32 = jnp.int32
ROW_DIMS = (((1,), (1,)), ((), ()))
COL_DIMS = (((0,), (0,)), ((), ()))
VMEM = pl.BlockSpec(memory_space=pltpu.VMEM)
SMEM = pl.BlockSpec(memory_space=pltpu.SMEM)
HBM = pl.BlockSpec(memory_space=pltpu.HBM)


def peer(index, step, size):
    if size & (size - 1) == 0:
        return index ^ step
    return (index + step) % size


def power(exponent):
    return jnp.exp2(exponent).astype(BF16).astype(F32)


def iota(shape, dim):
    return lax.broadcasted_iota(I32, shape, dim)


def shaped(shape, dtype):
    return jax.ShapeDtypeStruct(shape, dtype)


def params(mib):
    return pltpu.CompilerParams(vmem_limit_bytes=mib * MIB)


def cost(flops, size):
    return pl.CostEstimate(flops=flops, bytes_accessed=size, transcendentals=0)


def in_hbm(array):
    return pltpu.with_memory_space_constraint(array, pltpu.HBM)


def as_lanes(column):
    rows = column.shape[0]
    wide = jnp.broadcast_to(column, (rows, 128))
    return jnp.transpose(jnp.concatenate([wide, jnp.zeros((128 - rows, 128), F32)], axis=0))[0:1, :]


def coded_rows(values):
    largest = jnp.maximum(jnp.max(jnp.abs(values), axis=1, keepdims=True), 2.0**-80)
    exponent = jnp.ceil(jnp.log2(largest) + 0.001) - 15.0
    return jnp.round(values * power(-exponent)).astype(I32), exponent


def turned_weights(weights):
    return jnp.transpose(jnp.broadcast_to(weights, (128, 128)))


def movers_kernel(n_groups, lists_group, list_ref, pos_ref, counts_ref, keep_ref, vec_ref, *refs):
    steps = n_groups - 1
    alive_ref, meta_ref, picks_ref = refs[:3]
    head_refs, row_refs = refs[3 : 3 + steps], refs[3 + steps : 3 + 2 * steps]
    lists, pos, fill, held, sems = refs[3 + 2 * steps :]
    loads = [
        pltpu.make_async_copy(src, dst, sems.at[steps + i])
        for i, (src, dst) in enumerate([(list_ref, lists), (pos_ref, pos), (counts_ref, fill), (keep_ref, held)])
    ]
    for load in loads:
        load.start()
    blocks, block = keep_ref.shape
    group = lax.axis_index("grp")
    base = (group * lax.axis_size("row") + lax.axis_index("row")) * blocks
    shift = lists_group.bit_length() - 1
    lane = iota((1, block), 1)
    row = iota((blocks, block), 0)
    slots = jnp.full((1, block), -1, I32)
    filled = jnp.zeros((blocks, block), I32)
    picks = [jnp.int32(-1)] * steps
    homes = [jnp.int32(-1)] * steps
    for load in loads[:2]:
        load.wait()
    for b in range(blocks):
        home = pos[lists[base + b]]
        home_group = home >> shift if lists_group == 1 << shift else home // lists_group
        slot = home - home_group * lists_group
        slots = jnp.where((lane == b) & (home_group == group), slot, slots)
        for k in range(steps):
            hit = home_group == peer(group, k + 1, n_groups)
            picks[k] = jnp.where(hit, b, picks[k])
            homes[k] = jnp.where(hit, slot, homes[k])
    fetches = []
    for k in range(steps):
        picks_ref[k] = picks[k]
        start = pl.multiple_of(jnp.maximum(picks[k], 0) * block, block)
        fetches.append(pltpu.make_async_copy(vec_ref.at[pl.ds(start, block), :], row_refs[k], sems.at[k]))
        fetches[k].start()
    for load in loads[2:]:
        load.wait()
    for b in range(blocks):
        filled = jnp.where(row == b, fill[b], filled)
    alive = held[...].astype(F32) * (iota((blocks, block), 1) < filled).astype(F32)
    alive_ref[...] = alive
    ones = jnp.ones((8, block), BF16)
    block_counts = lax.dot_general(ones, alive.astype(BF16), ROW_DIMS, preferred_element_type=F32)
    meta_ref[...] = jnp.zeros_like(meta_ref)
    meta_ref[0:1, :] = slots.astype(F32)
    meta_ref[1:2, 0:blocks] = block_counts[0:1, :]
    for k in range(steps):
        fetches[k].wait()
        weights = alive_ref[pl.ds(jnp.maximum(picks[k], 0), 1), :]
        wide = jnp.broadcast_to(weights, (16, block)).astype(BF16)
        total = jnp.dot(wide, row_refs[k][...], preferred_element_type=F32)
        chunks = total.shape[1] // 128
        for j in range(chunks):
            head_refs[k][j : j + 1, :] = total[0:1, j * 128 : (j + 1) * 128]
        head_refs[k][chunks : chunks + 8, :] = jnp.concatenate(
            [
                jnp.broadcast_to(jnp.sum(weights, axis=1, keepdims=True), (1, 128)),
                jnp.broadcast_to(homes[k].astype(F32), (1, 128)),
                jnp.zeros((6, 128), F32),
            ],
            axis=0,
        )


def movers(n_groups, lists_group, block_list, home_pos, counts, keep, vectors):
    steps = n_groups - 1
    blocks, block = keep.shape
    width = vectors.shape[1]
    outs = pl.pallas_call(
        functools.partial(movers_kernel, n_groups, lists_group),
        out_shape=[shaped((blocks, block), F32), shaped((8, block), F32), shaped((steps,), I32)]
        + [shaped((width // 128 + 8, 128), F32)] * steps
        + [shaped((block, width), BF16)] * steps,
        in_specs=[HBM] * 5,
        out_specs=[VMEM, VMEM, SMEM] + [VMEM] * (2 * steps),
        scratch_shapes=[
            pltpu.SMEM(block_list.shape, I32),
            pltpu.SMEM(home_pos.shape, I32),
            pltpu.SMEM(counts.shape, I32),
            pltpu.VMEM(keep.shape, I32),
            pltpu.SemaphoreType.DMA((steps + 4,)),
        ],
        compiler_params=params(8),
        cost_estimate=cost(2 * steps * block * width, 6 * steps * block * width),
        name="movers",
    )(*map(in_hbm, (block_list, home_pos, counts, keep, vectors)))
    return outs[0], outs[1], outs[2], outs[3 : 3 + steps], outs[3 + steps :]


def sums_kernel(alive_ref, vec_ref, sums_ref):
    blocks, block = alive_ref.shape
    tile = 8
    row = iota((tile, block), 0)
    for t in range(blocks // tile):
        alive = alive_ref[t * tile : (t + 1) * tile, :]
        spread = jnp.concatenate([jnp.where(row == j, alive, 0.0) for j in range(tile)], axis=1)
        rows = vec_ref[t * tile * block : (t + 1) * tile * block, :]
        sums_ref[t * tile : (t + 1) * tile, :] = jnp.dot(spread.astype(BF16), rows, preferred_element_type=F32)


def block_sums(alive, vectors):
    blocks = alive.shape[0]
    rows, width = vectors.shape
    return pl.pallas_call(
        sums_kernel,
        out_shape=shaped((blocks, width), F32),
        in_specs=[VMEM] * 2,
        out_specs=VMEM,
        compiler_params=params(16),
        cost_estimate=cost(16 * rows * width, 2 * rows * width),
        name="block_sums",
    )(alive, vectors)


def pack_kernel(meta_ref, sums_ref, *refs):
    heads, out_ref = refs[:-1][::-1], refs[-1]
    blocks, width = sums_ref.shape
    chunks = width // 128
    lane = iota((1, 128), 1)
    slots, counts = meta_ref[0:1, :], meta_ref[1:2, :]
    arrived = []
    for k, head in enumerate(heads):
        arrived.append(jnp.concatenate([head[j : j + 1, :] for j in range(chunks)], axis=1))
        slots = jnp.where(lane == blocks + k, head[chunks + 1 : chunks + 2, :], slots)
        counts = jnp.where(lane == blocks + k, head[chunks : chunks + 1, :], counts)
    coded, exponent = coded_rows(jnp.concatenate([sums_ref[...]] + arrived, axis=0))
    facts = jnp.concatenate([slots, counts, as_lanes(exponent)], axis=1).astype(I32)
    facts = jnp.concatenate([facts, jnp.zeros((1, width - 384), I32)], axis=1)
    tail = jnp.concatenate([coded[blocks:]] + [jnp.zeros((1, width), I32)] * (TAIL - 1 - len(heads)) + [facts], axis=0)
    parts = [coded[j : j + 8] for j in range(0, blocks, 8)]
    parts.append(jnp.concatenate([tail[:, : width // 2], tail[:, width // 2 :]], axis=0))
    out_ref[...] = jnp.concatenate(parts, axis=1).astype(I16)


def pack(meta, sums, heads):
    blocks, width = sums.shape
    size = blocks // 8 * width + width // 2
    return pl.pallas_call(
        pack_kernel,
        out_shape=shaped((8, size), I16),
        in_specs=[VMEM] * (2 + len(heads)),
        out_specs=VMEM,
        compiler_params=params(8),
        cost_estimate=cost(6 * 10**9, 48 * size),
        name="pack",
    )(meta, sums, *heads[::-1])


def unpacked(packed, blocks, width):
    big = jnp.concatenate([packed[:, j * width : (j + 1) * width] for j in range(blocks // 8)], axis=0)
    tail = packed[:, blocks // 8 * width :]
    return big, jnp.concatenate([tail[:TAIL], tail[TAIL:]], axis=1)


def add_up(sources, blocks, lists, width):
    sources = [unpacked(x, blocks, width) for x in sources]
    fill = len(sources) % 2
    big = jnp.concatenate([x for x, _ in sources], axis=0)
    small = jnp.concatenate([x for _, x in sources] + [jnp.zeros((TAIL, width), I32)] * fill, axis=0)

    def lanes(which, spare):
        facts = [x[TAIL - 1 :, 128 * which : 128 * which + 128].astype(F32) for _, x in sources]
        wide = jnp.concatenate([x[:, 0:blocks] for x in facts], axis=1)
        tail = [x[:, blocks : blocks + TAIL] for x in facts] + [jnp.full((1, TAIL), spare, F32)] * fill
        return wide, jnp.concatenate(tail, axis=1)

    def four(pair, low=True):
        wide, tail = pair
        return jnp.concatenate([wide, wide * low, tail, tail * low], axis=1)

    slots = four(lanes(0, -1.0))
    counts = four(lanes(1, 0.0), low=False)
    scale, scale_small = map(power, lanes(2, 0.0))
    scale = jnp.concatenate([256.0 * scale, scale, 256.0 * scale_small, scale_small], axis=1)
    hit = iota((lists, slots.shape[1]), 0) == slots.astype(I32)
    totals = jnp.sum(jnp.where(hit, counts, 0.0), axis=1, keepdims=True)
    values = jnp.concatenate([big >> 8, big & 255, small >> 8, small & 255], axis=0)
    sums = jnp.dot(
        jnp.where(hit, scale, 0.0).astype(BF16), values.astype(F32).astype(BF16), preferred_element_type=F32
    )
    return sums, totals


def prior_kernel(blocks, *refs):
    near, (old_ref, sums_ref, totals_ref) = refs[:-3], refs[-3:]
    lists = old_ref.shape[0]
    prior = 1.0 * PRIOR
    sums, totals = add_up([ref[...].astype(I32) for ref in near], blocks, lists, old_ref.shape[1])
    sums_ref[...] = sums + prior * old_ref[...].astype(F32)
    totals_ref[...] = jnp.broadcast_to(totals + prior, totals_ref.shape)


def with_prior(blocks, near, old):
    lists, width = old.shape
    return pl.pallas_call(
        functools.partial(prior_kernel, blocks),
        out_shape=[shaped((lists, width), F32), shaped((lists, 128), F32)],
        in_specs=[VMEM] * (1 + len(near)),
        out_specs=[VMEM] * 2,
        compiler_params=params(16),
        cost_estimate=cost(20000 * lists * width, 8 * lists * width),
        name="prior",
    )(*near, old)


def table_kernel(blocks, far, sums_ref, totals_ref, table_ref, norms_ref, share_ref):
    lists, width = sums_ref.shape
    far_all = far[...].astype(I32)
    sources = [far_all[j : j + 8] for j in range(0, far.shape[0], 8)]
    sums, totals = add_up(sources, blocks, lists, width)
    totals = totals_ref[:, 0:1] + totals
    table = ((sums_ref[...] + sums) * (1.0 / totals)).astype(BF16)
    table_ref[...] = table
    share = share_ref.shape[0]
    start = pl.multiple_of(lax.axis_index("row") * share, share)
    share_ref[...] = table_ref[pl.ds(start, share), :]
    squares = jnp.square(table.astype(F32))
    partial = squares[:, 0:128]
    for j in range(1, width // 128):
        partial = partial + squares[:, j * 128 : (j + 1) * 128]
    ones = jnp.ones((16, 128), BF16)
    norms = jnp.zeros((16, lists), F32)
    for _ in range(3):
        piece = partial.astype(BF16)
        partial = partial - piece.astype(F32)
        norms = norms + lax.dot_general(ones, piece, ROW_DIMS, preferred_element_type=F32)
    norms_ref[...] = norms[0:8] * (1.0 / math.sqrt(width))


def make_table(n_rows, blocks, far, sums, totals):
    lists, width = sums.shape
    return pl.pallas_call(
        functools.partial(table_kernel, blocks),
        out_shape=[shaped((lists, width), BF16), shaped((8, lists), F32), shaped((lists // n_rows, width), BF16)],
        in_specs=[VMEM] * 3,
        out_specs=[VMEM] * 3,
        compiler_params=params(24),
        cost_estimate=cost(2000 * lists * width, 8 * lists * width),
        name="table",
    )(far, sums, totals)


def parts_kernel(norms_ref, table_ref, *refs):
    steps = len(refs) // 2
    factor = 1.0 / math.sqrt(table_ref.shape[1])
    norms = norms_ref[0:1, :]
    for row_ref, part_ref in zip(refs[:steps], refs[steps:]):
        dots = lax.dot_general(row_ref[...], table_ref[...], ROW_DIMS, preferred_element_type=F32)
        part_ref[...] = (dots * (2.0 * factor) - norms).astype(part_ref.dtype)


def parts_of(norms, table, rows):
    lists, width = table.shape
    block = rows[0].shape[0]
    return pl.pallas_call(
        parts_kernel,
        out_shape=[shaped((block, lists), BF16)] * len(rows),
        in_specs=[VMEM] * (2 + len(rows)),
        out_specs=[VMEM] * len(rows),
        compiler_params=params(16),
        cost_estimate=cost(2 * len(rows) * block * lists * width, 2 * lists * width),
        name="parts",
    )(norms, table, *rows)


def scores_kernel(alive_ref, norms_ref, table_ref, vec_ref, out_ref, held, sems):
    blocks, block = alive_ref.shape
    lists, width = table_ref.shape
    factor = 1.0 / math.sqrt(width)
    norms = norms_ref[0:1, :]
    table = table_ref[...]
    tile = 4
    stores = []
    for t in range(blocks // tile):
        span = slice(t * tile * block, (t + 1) * tile * block)
        dots = lax.dot_general(vec_ref[span, :], table, ROW_DIMS, preferred_element_type=F32)
        for j in range(tile):
            b = t * tile + j
            weights = jnp.concatenate([turned_weights(alive_ref[b : b + 1, :])] * (lists // 128), axis=1)
            part = dots[j * block : (j + 1) * block, :]
            held[b * block : (b + 1) * block, :] = (part * (2.0 * factor) - norms) * weights
        stores.append(pltpu.make_async_copy(held.at[span, :], out_ref.at[span, :], sems.at[t]))
        stores[t].start()
    for store in stores:
        store.wait()


def scores_of(alive, norms, table, vectors):
    blocks = alive.shape[0]
    rows, width = vectors.shape
    lists = table.shape[0]
    return pl.pallas_call(
        scores_kernel,
        out_shape=shaped((rows, lists), F32),
        in_specs=[VMEM] * 4,
        out_specs=HBM,
        scratch_shapes=[pltpu.VMEM((rows, lists), F32), pltpu.SemaphoreType.DMA((blocks // 4,))],
        compiler_params=params(24),
        cost_estimate=cost(2 * lists * rows * width, 4 * rows * lists),
        name="scores",
    )(alive, norms, table, vectors)


def merge_kernel(picks_ref, alive_ref, *refs):
    steps = picks_ref.shape[0]
    parts, out_ref, held, sems = refs[:steps], refs[steps + 1], refs[steps + 2], refs[steps + 3]
    block, lists = parts[0].shape

    def store(k):
        start = pl.multiple_of(picks_ref[k] * block, block)
        return pltpu.make_async_copy(held.at[k], out_ref.at[pl.ds(start, block), :], sems.at[k])

    for k in range(steps):

        @pl.when(picks_ref[k] >= 0)
        def _():
            weights = turned_weights(alive_ref[pl.ds(picks_ref[k], 1), :])
            weights = jnp.concatenate([weights] * (lists // 128), axis=1)
            held[k] = parts[k][...].astype(F32) * weights
            store(k).start()

    for k in range(steps):

        @pl.when(picks_ref[k] >= 0)
        def _():
            store(k).wait()


def merge(picks, alive, parts, scores):
    steps = len(parts)
    block, lists = parts[0].shape
    return pl.pallas_call(
        merge_kernel,
        out_shape=shaped(scores.shape, scores.dtype),
        in_specs=[SMEM, VMEM] + [VMEM] * steps + [HBM],
        out_specs=HBM,
        scratch_shapes=[pltpu.VMEM((steps, block, lists), F32), pltpu.SemaphoreType.DMA((steps,))],
        input_output_aliases={2 + steps: 0},
        compiler_params=params(8),
        cost_estimate=cost(2 * steps * block * lists, 6 * steps * block * lists),
        name="merge",
    )(picks, alive, *parts, scores)


def local(vectors, keep_bits, counts, block_list, home_pos, old_centroids):
    n_groups = lax.axis_size("grp")
    n_rows = lax.axis_size("row")
    blocks = counts.shape[0]
    block = vectors.shape[0] // blocks
    lists_group = old_centroids.shape[0]
    keep = keep_bits.reshape(blocks, block)
    there = [[(i, peer(i, k, n_groups)) for i in range(n_groups)] for k in range(1, n_groups)]
    back = [[(j, i) for i, j in pairs] for pairs in there]
    chips = n_rows // 2
    along = [[(i, 2 * peer(i // 2, k, chips) + i % 2) for i in range(n_rows)] for k in range(1, chips)]
    cores = [(i, i ^ 1) for i in range(n_rows)]

    alive, meta, picks, heads, rows = movers(n_groups, lists_group, block_list, home_pos, counts, keep, vectors)
    heads = [lax.ppermute(x, "grp", pairs) for x, pairs in zip(heads[::-1], there[::-1])][::-1]
    sums = block_sums(alive, vectors)
    last = lax.ppermute(rows[-1], "grp", there[-1])
    mine = pack(meta, sums, heads)
    mine, *rows = lax.optimization_barrier((mine, *rows[:-1]))
    rows = [lax.ppermute(x, "grp", pairs) for x, pairs in zip(rows, there)]
    order = sorted(range(chips - 1), key=lambda i: (i + 1 == chips - 1, i == 0))
    near = [lax.ppermute(mine, "row", along[i]) for i in order]
    sums, totals = with_prior(blocks, [mine] + near, old_centroids)
    near, last = lax.optimization_barrier((near, last))
    both = jnp.concatenate([mine] + near, axis=0)
    rows.append(last)
    far = lax.ppermute(both, "row", cores)
    table, norms, share = make_table(n_rows, blocks, far, sums, totals)
    parts = parts_of(norms, table, rows)
    parts = [lax.ppermute(x, "grp", pairs) for x, pairs in zip(parts, back)]
    scores = scores_of(alive, norms, table, vectors)
    scores = merge(picks, alive, parts, scores)
    return (share, scores)


def solution(mesh):
    in_specs = (
        P(("grp", "row"), None),
        P(("grp", "row")),
        P(("grp", "row")),
        P(),
        P(),
        P("grp", None),
    )
    out_specs = (P(("grp", "row"), None), P(("grp", "row"), None))
    return jax.shard_map(local, mesh=mesh, in_specs=in_specs, out_specs=out_specs, check_vma=False)
```

```python
import functools
import math

import jax
import jax.numpy as jnp
from jax import lax
from jax.experimental import pallas as pl
from jax.experimental.pallas import tpu as pltpu
from jax.sharding import PartitionSpec as P

PRIOR = 16
TAIL = 4
MIB = 1 << 20
F32 = jnp.float32
BF16 = jnp.bfloat16
I16 = jnp.int16
I32 = jnp.int32
ROW_DIMS = (((1,), (1,)), ((), ()))
COL_DIMS = (((0,), (0,)), ((), ()))
VMEM = pl.BlockSpec(memory_space=pltpu.VMEM)
SMEM = pl.BlockSpec(memory_space=pltpu.SMEM)
HBM = pl.BlockSpec(memory_space=pltpu.HBM)


def peer(index, step, size):
    if size & (size - 1) == 0:
        return index ^ step
    return (index + step) % size


def power(exponent):
    return jnp.exp2(exponent).astype(BF16).astype(F32)


def iota(shape, dim):
    return lax.broadcasted_iota(I32, shape, dim)


def shaped(shape, dtype):
    return jax.ShapeDtypeStruct(shape, dtype)


def params(mib):
    return pltpu.CompilerParams(vmem_limit_bytes=mib * MIB)


def cost(flops, size):
    return pl.CostEstimate(flops=flops, bytes_accessed=size, transcendentals=0)


def in_hbm(array):
    return pltpu.with_memory_space_constraint(array, pltpu.HBM)


def as_lanes(column):
    rows = column.shape[0]
    wide = jnp.broadcast_to(column, (rows, 128))
    return jnp.transpose(jnp.concatenate([wide, jnp.zeros((128 - rows, 128), F32)], axis=0))[0:1, :]


def coded_rows(values):
    largest = jnp.maximum(jnp.max(jnp.abs(values), axis=1, keepdims=True), 2.0**-80)
    exponent = jnp.ceil(jnp.log2(largest) + 0.001) - 15.0
    return jnp.round(values * power(-exponent)).astype(I32), exponent


def turned_weights(weights):
    return jnp.transpose(jnp.broadcast_to(weights, (128, 128)))


def movers_kernel(n_groups, lists_group, list_ref, pos_ref, counts_ref, keep_ref, vec_ref, *refs):
    steps = n_groups - 1
    alive_ref, meta_ref, picks_ref = refs[:3]
    head_refs, row_refs = refs[3 : 3 + steps], refs[3 + steps : 3 + 2 * steps]
    lists, pos, fill, held, sems = refs[3 + 2 * steps :]
    loads = [
        pltpu.make_async_copy(src, dst, sems.at[steps + i])
        for i, (src, dst) in enumerate([(list_ref, lists), (pos_ref, pos), (counts_ref, fill), (keep_ref, held)])
    ]
    for load in loads:
        load.start()
    blocks, block = keep_ref.shape
    group = lax.axis_index("grp")
    base = (group * lax.axis_size("row") + lax.axis_index("row")) * blocks
    shift = lists_group.bit_length() - 1
    lane = iota((1, block), 1)
    row = iota((blocks, block), 0)
    slots = jnp.full((1, block), -1, I32)
    filled = jnp.zeros((blocks, block), I32)
    picks = [jnp.int32(-1)] * steps
    homes = [jnp.int32(-1)] * steps
    for load in loads[:2]:
        load.wait()
    for b in range(blocks):
        home = pos[lists[base + b]]
        home_group = home >> shift if lists_group == 1 << shift else home // lists_group
        slot = home - home_group * lists_group
        slots = jnp.where((lane == b) & (home_group == group), slot, slots)
        for k in range(steps):
            hit = home_group == peer(group, k + 1, n_groups)
            picks[k] = jnp.where(hit, b, picks[k])
            homes[k] = jnp.where(hit, slot, homes[k])
    fetches = []
    for k in range(steps):
        picks_ref[k] = picks[k]
        start = pl.multiple_of(jnp.maximum(picks[k], 0) * block, block)
        fetches.append(pltpu.make_async_copy(vec_ref.at[pl.ds(start, block), :], row_refs[k], sems.at[k]))
        fetches[k].start()
    for load in loads[2:]:
        load.wait()
    for b in range(blocks):
        filled = jnp.where(row == b, fill[b], filled)
    alive = held[...].astype(F32) * (iota((blocks, block), 1) < filled).astype(F32)
    alive_ref[...] = alive
    ones = jnp.ones((8, block), BF16)
    block_counts = lax.dot_general(ones, alive.astype(BF16), ROW_DIMS, preferred_element_type=F32)
    meta_ref[...] = jnp.zeros_like(meta_ref)
    meta_ref[0:1, :] = slots.astype(F32)
    meta_ref[1:2, 0:blocks] = block_counts[0:1, :]
    for k in range(steps):
        fetches[k].wait()
        weights = alive_ref[pl.ds(jnp.maximum(picks[k], 0), 1), :]
        wide = jnp.broadcast_to(weights, (16, block)).astype(BF16)
        total = jnp.dot(wide, row_refs[k][...], preferred_element_type=F32)
        chunks = total.shape[1] // 128
        for j in range(chunks):
            head_refs[k][j : j + 1, :] = total[0:1, j * 128 : (j + 1) * 128]
        head_refs[k][chunks : chunks + 8, :] = jnp.concatenate(
            [
                jnp.broadcast_to(jnp.sum(weights, axis=1, keepdims=True), (1, 128)),
                jnp.broadcast_to(homes[k].astype(F32), (1, 128)),
                jnp.zeros((6, 128), F32),
            ],
            axis=0,
        )


def movers(n_groups, lists_group, block_list, home_pos, counts, keep, vectors):
    steps = n_groups - 1
    blocks, block = keep.shape
    width = vectors.shape[1]
    outs = pl.pallas_call(
        functools.partial(movers_kernel, n_groups, lists_group),
        out_shape=[shaped((blocks, block), F32), shaped((8, block), F32), shaped((steps,), I32)]
        + [shaped((width // 128 + 8, 128), F32)] * steps
        + [shaped((block, width), BF16)] * steps,
        in_specs=[HBM] * 5,
        out_specs=[VMEM, VMEM, SMEM] + [VMEM] * (2 * steps),
        scratch_shapes=[
            pltpu.SMEM(block_list.shape, I32),
            pltpu.SMEM(home_pos.shape, I32),
            pltpu.SMEM(counts.shape, I32),
            pltpu.VMEM(keep.shape, I32),
            pltpu.SemaphoreType.DMA((steps + 4,)),
        ],
        compiler_params=params(8),
        cost_estimate=cost(2 * steps * block * width, 6 * steps * block * width),
        name="movers",
    )(*map(in_hbm, (block_list, home_pos, counts, keep, vectors)))
    return outs[0], outs[1], outs[2], outs[3 : 3 + steps], outs[3 + steps :]


def sums_kernel(alive_ref, vec_ref, sums_ref):
    blocks, block = alive_ref.shape
    tile = 8
    row = iota((tile, block), 0)
    for t in range(blocks // tile):
        alive = alive_ref[t * tile : (t + 1) * tile, :]
        spread = jnp.concatenate([jnp.where(row == j, alive, 0.0) for j in range(tile)], axis=1)
        rows = vec_ref[t * tile * block : (t + 1) * tile * block, :]
        sums_ref[t * tile : (t + 1) * tile, :] = jnp.dot(spread.astype(BF16), rows, preferred_element_type=F32)


def block_sums(alive, vectors):
    blocks = alive.shape[0]
    rows, width = vectors.shape
    return pl.pallas_call(
        sums_kernel,
        out_shape=shaped((blocks, width), F32),
        in_specs=[VMEM] * 2,
        out_specs=VMEM,
        compiler_params=params(16),
        cost_estimate=cost(16 * rows * width, 2 * rows * width),
        name="block_sums",
    )(alive, vectors)


def pack_kernel(meta_ref, sums_ref, *refs):
    heads, out_ref = refs[:-1][::-1], refs[-1]
    blocks, width = sums_ref.shape
    chunks = width // 128
    lane = iota((1, 128), 1)
    slots, counts = meta_ref[0:1, :], meta_ref[1:2, :]
    arrived = []
    for k, head in enumerate(heads):
        arrived.append(jnp.concatenate([head[j : j + 1, :] for j in range(chunks)], axis=1))
        slots = jnp.where(lane == blocks + k, head[chunks + 1 : chunks + 2, :], slots)
        counts = jnp.where(lane == blocks + k, head[chunks : chunks + 1, :], counts)
    coded, exponent = coded_rows(jnp.concatenate([sums_ref[...]] + arrived, axis=0))
    facts = jnp.concatenate([slots, counts, as_lanes(exponent)], axis=1).astype(I32)
    facts = jnp.concatenate([facts, jnp.zeros((1, width - 384), I32)], axis=1)
    tail = jnp.concatenate([coded[blocks:]] + [jnp.zeros((1, width), I32)] * (TAIL - 1 - len(heads)) + [facts], axis=0)
    parts = [coded[j : j + 8] for j in range(0, blocks, 8)]
    parts.append(jnp.concatenate([tail[:, : width // 2], tail[:, width // 2 :]], axis=0))
    out_ref[...] = jnp.concatenate(parts, axis=1).astype(I16)


def pack(meta, sums, heads):
    blocks, width = sums.shape
    size = blocks // 8 * width + width // 2
    return pl.pallas_call(
        pack_kernel,
        out_shape=shaped((8, size), I16),
        in_specs=[VMEM] * (2 + len(heads)),
        out_specs=VMEM,
        compiler_params=params(8),
        cost_estimate=cost(6 * 10**9, 48 * size),
        name="pack",
    )(meta, sums, *heads[::-1])


def unpacked(packed, blocks, width):
    big = jnp.concatenate([packed[:, j * width : (j + 1) * width] for j in range(blocks // 8)], axis=0)
    tail = packed[:, blocks // 8 * width :]
    return big, jnp.concatenate([tail[:TAIL], tail[TAIL:]], axis=1)


def add_up(sources, blocks, lists, width):
    sources = [unpacked(x, blocks, width) for x in sources]
    fill = len(sources) % 2
    big = jnp.concatenate([x for x, _ in sources], axis=0)
    small = jnp.concatenate([x for _, x in sources] + [jnp.zeros((TAIL, width), I32)] * fill, axis=0)

    def lanes(which, spare):
        facts = [x[TAIL - 1 :, 128 * which : 128 * which + 128].astype(F32) for _, x in sources]
        wide = jnp.concatenate([x[:, 0:blocks] for x in facts], axis=1)
        tail = [x[:, blocks : blocks + TAIL] for x in facts] + [jnp.full((1, TAIL), spare, F32)] * fill
        return wide, jnp.concatenate(tail, axis=1)

    def four(pair, low=True):
        wide, tail = pair
        return jnp.concatenate([wide, wide * low, tail, tail * low], axis=1)

    slots = four(lanes(0, -1.0))
    counts = four(lanes(1, 0.0), low=False)
    scale, scale_small = map(power, lanes(2, 0.0))
    scale = jnp.concatenate([256.0 * scale, scale, 256.0 * scale_small, scale_small], axis=1)
    hit = iota((lists, slots.shape[1]), 0) == slots.astype(I32)
    totals = jnp.sum(jnp.where(hit, counts, 0.0), axis=1, keepdims=True)
    values = jnp.concatenate([big >> 8, big & 255, small >> 8, small & 255], axis=0)
    sums = jnp.dot(
        jnp.where(hit, scale, 0.0).astype(BF16), values.astype(F32).astype(BF16), preferred_element_type=F32
    )
    return sums, totals


def prior_kernel(blocks, *refs):
    near, (old_ref, sums_ref, totals_ref) = refs[:-3], refs[-3:]
    lists = old_ref.shape[0]
    prior = 1.0 * PRIOR
    sums, totals = add_up([ref[...].astype(I32) for ref in near], blocks, lists, old_ref.shape[1])
    sums_ref[...] = sums + prior * old_ref[...].astype(F32)
    totals_ref[...] = jnp.broadcast_to(totals + prior, totals_ref.shape)


def with_prior(blocks, near, old):
    lists, width = old.shape
    return pl.pallas_call(
        functools.partial(prior_kernel, blocks),
        out_shape=[shaped((lists, width), F32), shaped((lists, 128), F32)],
        in_specs=[VMEM] * (1 + len(near)),
        out_specs=[VMEM] * 2,
        compiler_params=params(16),
        cost_estimate=cost(20000 * lists * width, 8 * lists * width),
        name="prior",
    )(*near, old)


def table_kernel(blocks, far, sums_ref, totals_ref, row_ref, table_ref, norms_ref, share_ref, part_ref):
    lists, width = sums_ref.shape
    far_all = far[...].astype(I32)
    sources = [far_all[j : j + 8] for j in range(0, far.shape[0], 8)]
    sums, totals = add_up(sources, blocks, lists, width)
    totals = totals_ref[:, 0:1] + totals
    table = ((sums_ref[...] + sums) * (1.0 / totals)).astype(BF16)
    table_ref[...] = table
    share = share_ref.shape[0]
    start = pl.multiple_of(lax.axis_index("row") * share, share)
    share_ref[...] = table_ref[pl.ds(start, share), :]
    squares = jnp.square(table.astype(F32))
    partial = squares[:, 0:128]
    for j in range(1, width // 128):
        partial = partial + squares[:, j * 128 : (j + 1) * 128]
    ones = jnp.ones((16, 128), BF16)
    norms = jnp.zeros((16, lists), F32)
    for _ in range(3):
        piece = partial.astype(BF16)
        partial = partial - piece.astype(F32)
        norms = norms + lax.dot_general(ones, piece, ROW_DIMS, preferred_element_type=F32)
    factor = 1.0 / math.sqrt(width)
    norms = norms * factor
    norms_ref[...] = norms[0:8]
    dots = lax.dot_general(row_ref[...], table, ROW_DIMS, preferred_element_type=F32)
    part_ref[...] = (dots * (2.0 * factor) - norms[0:1, :]).astype(part_ref.dtype)


def make_table(n_rows, blocks, far, sums, totals, rows):
    lists, width = sums.shape
    return pl.pallas_call(
        functools.partial(table_kernel, blocks),
        out_shape=[
            shaped((lists, width), BF16),
            shaped((8, lists), F32),
            shaped((lists // n_rows, width), BF16),
            shaped((rows.shape[0], lists), BF16),
        ],
        in_specs=[VMEM] * 4,
        out_specs=[VMEM] * 4,
        compiler_params=params(24),
        cost_estimate=cost(2000 * lists * width, 8 * lists * width),
        name="table",
    )(far, sums, totals, rows)


def parts_kernel(norms_ref, table_ref, *refs):
    steps = len(refs) // 2
    factor = 1.0 / math.sqrt(table_ref.shape[1])
    norms = norms_ref[0:1, :]
    for row_ref, part_ref in zip(refs[:steps], refs[steps:]):
        dots = lax.dot_general(row_ref[...], table_ref[...], ROW_DIMS, preferred_element_type=F32)
        part_ref[...] = (dots * (2.0 * factor) - norms).astype(part_ref.dtype)


def parts_of(norms, table, rows):
    lists, width = table.shape
    block = rows[0].shape[0]
    return pl.pallas_call(
        parts_kernel,
        out_shape=[shaped((block, lists), BF16)] * len(rows),
        in_specs=[VMEM] * (2 + len(rows)),
        out_specs=[VMEM] * len(rows),
        compiler_params=params(16),
        cost_estimate=cost(2 * len(rows) * block * lists * width, 2 * lists * width),
        name="parts",
    )(norms, table, *rows)


def scores_kernel(alive_ref, norms_ref, table_ref, vec_ref, out_ref, held, sems):
    blocks, block = alive_ref.shape
    lists, width = table_ref.shape
    factor = 1.0 / math.sqrt(width)
    norms = norms_ref[0:1, :]
    table = table_ref[...]
    tile = 4
    stores = []
    for t in range(blocks // tile):
        span = slice(t * tile * block, (t + 1) * tile * block)
        dots = lax.dot_general(vec_ref[span, :], table, ROW_DIMS, preferred_element_type=F32)
        for j in range(tile):
            b = t * tile + j
            weights = jnp.concatenate([turned_weights(alive_ref[b : b + 1, :])] * (lists // 128), axis=1)
            part = dots[j * block : (j + 1) * block, :]
            held[b * block : (b + 1) * block, :] = (part * (2.0 * factor) - norms) * weights
        stores.append(pltpu.make_async_copy(held.at[span, :], out_ref.at[span, :], sems.at[t]))
        stores[t].start()
    for store in stores:
        store.wait()


def scores_of(alive, norms, table, vectors):
    blocks = alive.shape[0]
    rows, width = vectors.shape
    lists = table.shape[0]
    return pl.pallas_call(
        scores_kernel,
        out_shape=shaped((rows, lists), F32),
        in_specs=[VMEM] * 4,
        out_specs=HBM,
        scratch_shapes=[pltpu.VMEM((rows, lists), F32), pltpu.SemaphoreType.DMA((blocks // 4,))],
        compiler_params=params(24),
        cost_estimate=cost(2 * lists * rows * width, 4 * rows * lists),
        name="scores",
    )(alive, norms, table, vectors)


def merge_kernel(picks_ref, alive_ref, *refs):
    steps = picks_ref.shape[0]
    parts, out_ref, held, sems = refs[:steps], refs[steps + 1], refs[steps + 2], refs[steps + 3]
    block, lists = parts[0].shape

    def store(k):
        start = pl.multiple_of(picks_ref[k] * block, block)
        return pltpu.make_async_copy(held.at[k], out_ref.at[pl.ds(start, block), :], sems.at[k])

    for k in range(steps):

        @pl.when(picks_ref[k] >= 0)
        def _():
            weights = turned_weights(alive_ref[pl.ds(picks_ref[k], 1), :])
            weights = jnp.concatenate([weights] * (lists // 128), axis=1)
            held[k] = parts[k][...].astype(F32) * weights
            store(k).start()

    for k in range(steps):

        @pl.when(picks_ref[k] >= 0)
        def _():
            store(k).wait()


def merge(picks, alive, parts, scores):
    steps = len(parts)
    block, lists = parts[0].shape
    return pl.pallas_call(
        merge_kernel,
        out_shape=shaped(scores.shape, scores.dtype),
        in_specs=[SMEM, VMEM] + [VMEM] * steps + [HBM],
        out_specs=HBM,
        scratch_shapes=[pltpu.VMEM((steps, block, lists), F32), pltpu.SemaphoreType.DMA((steps,))],
        input_output_aliases={2 + steps: 0},
        compiler_params=params(8),
        cost_estimate=cost(2 * steps * block * lists, 6 * steps * block * lists),
        name="merge",
    )(picks, alive, *parts, scores)


def local(vectors, keep_bits, counts, block_list, home_pos, old_centroids):
    n_groups = lax.axis_size("grp")
    n_rows = lax.axis_size("row")
    blocks = counts.shape[0]
    block = vectors.shape[0] // blocks
    lists_group = old_centroids.shape[0]
    keep = keep_bits.reshape(blocks, block)
    there = [[(i, peer(i, k, n_groups)) for i in range(n_groups)] for k in range(1, n_groups)]
    back = [[(j, i) for i, j in pairs] for pairs in there]
    chips = n_rows // 2
    along = [[(i, 2 * peer(i // 2, k, chips) + i % 2) for i in range(n_rows)] for k in range(1, chips)]
    cores = [(i, i ^ 1) for i in range(n_rows)]

    alive, meta, picks, heads, rows = movers(n_groups, lists_group, block_list, home_pos, counts, keep, vectors)
    heads = [lax.ppermute(x, "grp", pairs) for x, pairs in zip(heads[::-1], there[::-1])][::-1]
    sums = block_sums(alive, vectors)
    last = lax.ppermute(rows[-1], "grp", there[-1])
    mine = pack(meta, sums, heads)
    mine, *rows = lax.optimization_barrier((mine, *rows[:-1]))
    rows = [lax.ppermute(x, "grp", pairs) for x, pairs in zip(rows, there)]
    order = sorted(range(chips - 1), key=lambda i: (i + 1 == chips - 1, i == 0))
    near = [lax.ppermute(mine, "row", along[i]) for i in order]
    sums, totals = with_prior(blocks, [mine] + near, old_centroids)
    near, last = lax.optimization_barrier((near, last))
    both = jnp.concatenate([mine] + near, axis=0)
    rows.append(last)
    far = lax.ppermute(both, "row", cores)
    table, norms, share, part = make_table(n_rows, blocks, far, sums, totals, rows[-1])
    parts = [*parts_of(norms, table, rows[:-1]), part]
    parts = [lax.ppermute(x, "grp", pairs) for x, pairs in zip(parts, back)]
    scores = scores_of(alive, norms, table, vectors)
    scores = merge(picks, alive, parts, scores)
    return (share, scores)


def solution(mesh):
    in_specs = (
        P(("grp", "row"), None),
        P(("grp", "row")),
        P(("grp", "row")),
        P(),
        P(),
        P("grp", None),
    )
    out_specs = (P(("grp", "row"), None), P(("grp", "row"), None))
    return jax.shard_map(local, mesh=mesh, in_specs=in_specs, out_specs=out_specs, check_vma=False)
```

```python
import functools
import math

import jax
import jax.numpy as jnp
from jax import lax
from jax.experimental import pallas as pl
from jax.experimental.pallas import tpu as pltpu
from jax.sharding import PartitionSpec as P

PRIOR = 16
TAIL = 4
MIB = 1 << 20
F32 = jnp.float32
BF16 = jnp.bfloat16
I16 = jnp.int16
I32 = jnp.int32
ROW_DIMS = (((1,), (1,)), ((), ()))
COL_DIMS = (((0,), (0,)), ((), ()))
VMEM = pl.BlockSpec(memory_space=pltpu.VMEM)
SMEM = pl.BlockSpec(memory_space=pltpu.SMEM)
HBM = pl.BlockSpec(memory_space=pltpu.HBM)


def peer(index, step, size):
    if size & (size - 1) == 0:
        return index ^ step
    return (index + step) % size


def power(exponent):
    return jnp.exp2(exponent).astype(BF16).astype(F32)


def iota(shape, dim):
    return lax.broadcasted_iota(I32, shape, dim)


def shaped(shape, dtype):
    return jax.ShapeDtypeStruct(shape, dtype)


def params(mib):
    return pltpu.CompilerParams(vmem_limit_bytes=mib * MIB)


def cost(flops, size):
    return pl.CostEstimate(flops=flops, bytes_accessed=size, transcendentals=0)


def in_hbm(array):
    return pltpu.with_memory_space_constraint(array, pltpu.HBM)


def as_lanes(column):
    rows = column.shape[0]
    wide = jnp.broadcast_to(column, (rows, 128))
    return jnp.transpose(jnp.concatenate([wide, jnp.zeros((128 - rows, 128), F32)], axis=0))[0:1, :]


def coded_rows(values):
    largest = jnp.maximum(jnp.max(jnp.abs(values), axis=1, keepdims=True), 2.0**-80)
    exponent = jnp.ceil(jnp.log2(largest) + 0.001) - 15.0
    return jnp.round(values * power(-exponent)).astype(I32), exponent


def turned_weights(weights):
    return jnp.transpose(jnp.broadcast_to(weights, (128, 128)))


def movers_kernel(n_groups, lists_group, list_ref, pos_ref, counts_ref, keep_ref, vec_ref, *refs):
    steps = n_groups - 1
    alive_ref, meta_ref, picks_ref = refs[:3]
    head_refs, row_refs = refs[3 : 3 + steps], refs[3 + steps : 3 + 2 * steps]
    lists, pos, fill, held, sems = refs[3 + 2 * steps :]
    loads = [
        pltpu.make_async_copy(src, dst, sems.at[steps + i])
        for i, (src, dst) in enumerate([(list_ref, lists), (pos_ref, pos), (counts_ref, fill), (keep_ref, held)])
    ]
    for load in loads:
        load.start()
    blocks, block = keep_ref.shape
    group = lax.axis_index("grp")
    base = (group * lax.axis_size("row") + lax.axis_index("row")) * blocks
    shift = lists_group.bit_length() - 1
    lane = iota((1, block), 1)
    row = iota((blocks, block), 0)
    slots = jnp.full((1, block), -1, I32)
    filled = jnp.zeros((blocks, block), I32)
    picks = [jnp.int32(-1)] * steps
    homes = [jnp.int32(-1)] * steps
    for load in loads[:2]:
        load.wait()
    for b in range(blocks):
        home = pos[lists[base + b]]
        home_group = home >> shift if lists_group == 1 << shift else home // lists_group
        slot = home - home_group * lists_group
        slots = jnp.where((lane == b) & (home_group == group), slot, slots)
        for k in range(steps):
            hit = home_group == peer(group, k + 1, n_groups)
            picks[k] = jnp.where(hit, b, picks[k])
            homes[k] = jnp.where(hit, slot, homes[k])
    fetches = []
    for k in range(steps):
        picks_ref[k] = picks[k]
        start = pl.multiple_of(jnp.maximum(picks[k], 0) * block, block)
        fetches.append(pltpu.make_async_copy(vec_ref.at[pl.ds(start, block), :], row_refs[k], sems.at[k]))
        fetches[k].start()
    for load in loads[2:]:
        load.wait()
    for b in range(blocks):
        filled = jnp.where(row == b, fill[b], filled)
    alive = held[...].astype(F32) * (iota((blocks, block), 1) < filled).astype(F32)
    alive_ref[...] = alive
    ones = jnp.ones((8, block), BF16)
    block_counts = lax.dot_general(ones, alive.astype(BF16), ROW_DIMS, preferred_element_type=F32)
    meta_ref[...] = jnp.zeros_like(meta_ref)
    meta_ref[0:1, :] = slots.astype(F32)
    meta_ref[1:2, 0:blocks] = block_counts[0:1, :]
    for k in range(steps):
        fetches[k].wait()
        weights = alive_ref[pl.ds(jnp.maximum(picks[k], 0), 1), :]
        wide = jnp.broadcast_to(weights, (16, block)).astype(BF16)
        total = jnp.dot(wide, row_refs[k][...], preferred_element_type=F32)
        chunks = total.shape[1] // 128
        for j in range(chunks):
            head_refs[k][j : j + 1, :] = total[0:1, j * 128 : (j + 1) * 128]
        head_refs[k][chunks : chunks + 8, :] = jnp.concatenate(
            [
                jnp.broadcast_to(jnp.sum(weights, axis=1, keepdims=True), (1, 128)),
                jnp.broadcast_to(homes[k].astype(F32), (1, 128)),
                jnp.zeros((6, 128), F32),
            ],
            axis=0,
        )


def movers(n_groups, lists_group, block_list, home_pos, counts, keep, vectors):
    steps = n_groups - 1
    blocks, block = keep.shape
    width = vectors.shape[1]
    outs = pl.pallas_call(
        functools.partial(movers_kernel, n_groups, lists_group),
        out_shape=[shaped((blocks, block), F32), shaped((8, block), F32), shaped((steps,), I32)]
        + [shaped((width // 128 + 8, 128), F32)] * steps
        + [shaped((block, width), BF16)] * steps,
        in_specs=[HBM] * 5,
        out_specs=[VMEM, VMEM, SMEM] + [VMEM] * (2 * steps),
        scratch_shapes=[
            pltpu.SMEM(block_list.shape, I32),
            pltpu.SMEM(home_pos.shape, I32),
            pltpu.SMEM(counts.shape, I32),
            pltpu.VMEM(keep.shape, I32),
            pltpu.SemaphoreType.DMA((steps + 4,)),
        ],
        compiler_params=params(8),
        cost_estimate=cost(2 * steps * block * width, 6 * steps * block * width),
        name="movers",
    )(*map(in_hbm, (block_list, home_pos, counts, keep, vectors)))
    return outs[0], outs[1], outs[2], outs[3 : 3 + steps], outs[3 + steps :]


def sums_kernel(alive_ref, vec_ref, sums_ref):
    blocks, block = alive_ref.shape
    tile = 8
    row = iota((tile, block), 0)
    for t in range(blocks // tile):
        alive = alive_ref[t * tile : (t + 1) * tile, :]
        spread = jnp.concatenate([jnp.where(row == j, alive, 0.0) for j in range(tile)], axis=1)
        rows = vec_ref[t * tile * block : (t + 1) * tile * block, :]
        sums_ref[t * tile : (t + 1) * tile, :] = jnp.dot(spread.astype(BF16), rows, preferred_element_type=F32)


def block_sums(alive, vectors):
    blocks = alive.shape[0]
    rows, width = vectors.shape
    return pl.pallas_call(
        sums_kernel,
        out_shape=shaped((blocks, width), F32),
        in_specs=[VMEM] * 2,
        out_specs=VMEM,
        compiler_params=params(16),
        cost_estimate=cost(16 * rows * width, 2 * rows * width),
        name="block_sums",
    )(alive, vectors)


def pack_kernel(meta_ref, sums_ref, *refs):
    heads, out_ref = refs[:-1][::-1], refs[-1]
    blocks, width = sums_ref.shape
    chunks = width // 128
    lane = iota((1, 128), 1)
    slots, counts = meta_ref[0:1, :], meta_ref[1:2, :]
    arrived = []
    for k, head in enumerate(heads):
        arrived.append(jnp.concatenate([head[j : j + 1, :] for j in range(chunks)], axis=1))
        slots = jnp.where(lane == blocks + k, head[chunks + 1 : chunks + 2, :], slots)
        counts = jnp.where(lane == blocks + k, head[chunks : chunks + 1, :], counts)
    coded, exponent = coded_rows(jnp.concatenate([sums_ref[...]] + arrived, axis=0))
    facts = jnp.concatenate([slots, counts, as_lanes(exponent)], axis=1).astype(I32)
    facts = jnp.concatenate([facts, jnp.zeros((1, width - 384), I32)], axis=1)
    tail = jnp.concatenate([coded[blocks:]] + [jnp.zeros((1, width), I32)] * (TAIL - 1 - len(heads)) + [facts], axis=0)
    parts = [coded[j : j + 8] for j in range(0, blocks, 8)]
    parts.append(jnp.concatenate([tail[:, : width // 2], tail[:, width // 2 :]], axis=0))
    out_ref[...] = jnp.concatenate(parts, axis=1).astype(I16)


def pack(meta, sums, heads):
    blocks, width = sums.shape
    size = blocks // 8 * width + width // 2
    return pl.pallas_call(
        pack_kernel,
        out_shape=shaped((8, size), I16),
        in_specs=[VMEM] * (2 + len(heads)),
        out_specs=VMEM,
        compiler_params=params(8),
        cost_estimate=cost(6 * 10**9, 48 * size),
        name="pack",
    )(meta, sums, *heads[::-1])


def unpacked(packed, blocks, width):
    big = jnp.concatenate([packed[:, j * width : (j + 1) * width] for j in range(blocks // 8)], axis=0)
    tail = packed[:, blocks // 8 * width :]
    return big, jnp.concatenate([tail[:TAIL], tail[TAIL:]], axis=1)


def add_up(sources, blocks, lists, width):
    sources = [unpacked(x, blocks, width) for x in sources]
    fill = len(sources) % 2
    big = jnp.concatenate([x for x, _ in sources], axis=0)
    small = jnp.concatenate([x for _, x in sources] + [jnp.zeros((TAIL, width), I32)] * fill, axis=0)

    def lanes(which, spare):
        facts = [x[TAIL - 1 :, 128 * which : 128 * which + 128].astype(F32) for _, x in sources]
        wide = jnp.concatenate([x[:, 0:blocks] for x in facts], axis=1)
        tail = [x[:, blocks : blocks + TAIL] for x in facts] + [jnp.full((1, TAIL), spare, F32)] * fill
        return wide, jnp.concatenate(tail, axis=1)

    def four(pair, low=True):
        wide, tail = pair
        return jnp.concatenate([wide, wide * low, tail, tail * low], axis=1)

    slots = four(lanes(0, -1.0))
    counts = four(lanes(1, 0.0), low=False)
    scale, scale_small = map(power, lanes(2, 0.0))
    scale = jnp.concatenate([256.0 * scale, scale, 256.0 * scale_small, scale_small], axis=1)
    hit = iota((lists, slots.shape[1]), 0) == slots.astype(I32)
    totals = jnp.sum(jnp.where(hit, counts, 0.0), axis=1, keepdims=True)
    values = jnp.concatenate([big >> 8, big & 255, small >> 8, small & 255], axis=0)
    sums = jnp.dot(
        jnp.where(hit, scale, 0.0).astype(BF16), values.astype(F32).astype(BF16), preferred_element_type=F32
    )
    return sums, totals


def prior_kernel(blocks, *refs):
    near, (old_ref, sums_ref, totals_ref) = refs[:-3], refs[-3:]
    lists = old_ref.shape[0]
    prior = 1.0 * PRIOR
    sums, totals = add_up([ref[...].astype(I32) for ref in near], blocks, lists, old_ref.shape[1])
    sums_ref[...] = sums + prior * old_ref[...].astype(F32)
    totals_ref[...] = jnp.broadcast_to(totals + prior, totals_ref.shape)


def with_prior(blocks, near, old):
    lists, width = old.shape
    return pl.pallas_call(
        functools.partial(prior_kernel, blocks),
        out_shape=[shaped((lists, width), F32), shaped((lists, 128), F32)],
        in_specs=[VMEM] * (1 + len(near)),
        out_specs=[VMEM] * 2,
        compiler_params=params(16),
        cost_estimate=cost(20000 * lists * width, 8 * lists * width),
        name="prior",
    )(*near, old)


def table_kernel(blocks, far, sums_ref, totals_ref, row_ref, table_ref, norms_ref, share_ref, part_ref):
    lists, width = sums_ref.shape
    far_all = far[...].astype(I32)
    sources = [far_all[j : j + 8] for j in range(0, far.shape[0], 8)]
    sums, totals = add_up(sources, blocks, lists, width)
    totals = totals_ref[:, 0:1] + totals
    table = ((sums_ref[...] + sums) * (1.0 / totals)).astype(BF16)
    table_ref[...] = table
    share = share_ref.shape[0]
    start = pl.multiple_of(lax.axis_index("row") * share, share)
    share_ref[...] = table_ref[pl.ds(start, share), :]
    squares = jnp.square(table.astype(F32))
    partial = squares[:, 0:128]
    for j in range(1, width // 128):
        partial = partial + squares[:, j * 128 : (j + 1) * 128]
    ones = jnp.ones((16, 128), BF16)
    norms = jnp.zeros((16, lists), F32)
    for _ in range(3):
        piece = partial.astype(BF16)
        partial = partial - piece.astype(F32)
        norms = norms + lax.dot_general(ones, piece, ROW_DIMS, preferred_element_type=F32)
    factor = 1.0 / math.sqrt(width)
    norms = norms * factor
    norms_ref[...] = norms[0:8]
    dots = lax.dot_general(row_ref[...], table, ROW_DIMS, preferred_element_type=F32)
    part_ref[...] = (dots * (2.0 * factor) - norms[0:1, :]).astype(part_ref.dtype)


def make_table(n_rows, blocks, far, sums, totals, rows):
    lists, width = sums.shape
    return pl.pallas_call(
        functools.partial(table_kernel, blocks),
        out_shape=[
            shaped((lists, width), BF16),
            shaped((8, lists), F32),
            shaped((lists // n_rows, width), BF16),
            shaped((rows.shape[0], lists), BF16),
        ],
        in_specs=[VMEM] * 4,
        out_specs=[VMEM] * 4,
        compiler_params=params(24),
        cost_estimate=cost(2000 * lists * width, 8 * lists * width),
        name="table",
    )(far, sums, totals, rows)


def parts_kernel(norms_ref, table_ref, *refs):
    steps = len(refs) // 2
    factor = 1.0 / math.sqrt(table_ref.shape[1])
    norms = norms_ref[0:1, :]
    for row_ref, part_ref in zip(refs[:steps], refs[steps:]):
        dots = lax.dot_general(row_ref[...], table_ref[...], ROW_DIMS, preferred_element_type=F32)
        part_ref[...] = (dots * (2.0 * factor) - norms).astype(part_ref.dtype)


def parts_of(norms, table, rows):
    lists, width = table.shape
    block = rows[0].shape[0]
    return pl.pallas_call(
        parts_kernel,
        out_shape=[shaped((block, lists), BF16)] * len(rows),
        in_specs=[VMEM] * (2 + len(rows)),
        out_specs=[VMEM] * len(rows),
        compiler_params=params(16),
        cost_estimate=cost(2 * len(rows) * block * lists * width, 2 * lists * width),
        name="parts",
    )(norms, table, *rows)


def scores_kernel(alive_ref, norms_ref, table_ref, vec_ref, out_ref, held, sems):
    blocks, block = alive_ref.shape
    lists, width = table_ref.shape
    factor = 1.0 / math.sqrt(width)
    norms = norms_ref[0:1, :]
    table = table_ref[...]
    tile = 2
    stores = []
    for t in range(blocks // tile):
        span = slice(t * tile * block, (t + 1) * tile * block)
        dots = lax.dot_general(vec_ref[span, :], table, ROW_DIMS, preferred_element_type=F32)
        for j in range(tile):
            b = t * tile + j
            weights = jnp.concatenate([turned_weights(alive_ref[b : b + 1, :])] * (lists // 128), axis=1)
            part = dots[j * block : (j + 1) * block, :]
            held[b * block : (b + 1) * block, :] = (part * (2.0 * factor) - norms) * weights
        stores.append(pltpu.make_async_copy(held.at[span, :], out_ref.at[span, :], sems.at[t]))
        stores[t].start()
    for store in stores:
        store.wait()


def scores_of(alive, norms, table, vectors):
    blocks = alive.shape[0]
    rows, width = vectors.shape
    lists = table.shape[0]
    return pl.pallas_call(
        scores_kernel,
        out_shape=shaped((rows, lists), F32),
        in_specs=[VMEM] * 4,
        out_specs=HBM,
        scratch_shapes=[pltpu.VMEM((rows, lists), F32), pltpu.SemaphoreType.DMA((blocks // 2,))],
        compiler_params=params(24),
        cost_estimate=cost(2 * lists * rows * width, 4 * rows * lists),
        name="scores",
    )(alive, norms, table, vectors)


def merge_kernel(picks_ref, alive_ref, *refs):
    steps = picks_ref.shape[0]
    parts, out_ref, held, sems = refs[:steps], refs[steps + 1], refs[steps + 2], refs[steps + 3]
    block, lists = parts[0].shape

    def store(k):
        start = pl.multiple_of(picks_ref[k] * block, block)
        return pltpu.make_async_copy(held.at[k], out_ref.at[pl.ds(start, block), :], sems.at[k])

    for k in range(steps):

        @pl.when(picks_ref[k] >= 0)
        def _():
            weights = turned_weights(alive_ref[pl.ds(picks_ref[k], 1), :])
            weights = jnp.concatenate([weights] * (lists // 128), axis=1)
            held[k] = parts[k][...].astype(F32) * weights
            store(k).start()

    for k in range(steps):

        @pl.when(picks_ref[k] >= 0)
        def _():
            store(k).wait()


def merge(picks, alive, parts, scores):
    steps = len(parts)
    block, lists = parts[0].shape
    return pl.pallas_call(
        merge_kernel,
        out_shape=shaped(scores.shape, scores.dtype),
        in_specs=[SMEM, VMEM] + [VMEM] * steps + [HBM],
        out_specs=HBM,
        scratch_shapes=[pltpu.VMEM((steps, block, lists), F32), pltpu.SemaphoreType.DMA((steps,))],
        input_output_aliases={2 + steps: 0},
        compiler_params=params(8),
        cost_estimate=cost(2 * steps * block * lists, 6 * steps * block * lists),
        name="merge",
    )(picks, alive, *parts, scores)


def local(vectors, keep_bits, counts, block_list, home_pos, old_centroids):
    n_groups = lax.axis_size("grp")
    n_rows = lax.axis_size("row")
    blocks = counts.shape[0]
    block = vectors.shape[0] // blocks
    lists_group = old_centroids.shape[0]
    keep = keep_bits.reshape(blocks, block)
    there = [[(i, peer(i, k, n_groups)) for i in range(n_groups)] for k in range(1, n_groups)]
    back = [[(j, i) for i, j in pairs] for pairs in there]
    chips = n_rows // 2
    along = [[(i, 2 * peer(i // 2, k, chips) + i % 2) for i in range(n_rows)] for k in range(1, chips)]
    cores = [(i, i ^ 1) for i in range(n_rows)]

    alive, meta, picks, heads, rows = movers(n_groups, lists_group, block_list, home_pos, counts, keep, vectors)
    heads = [lax.ppermute(x, "grp", pairs) for x, pairs in zip(heads[::-1], there[::-1])][::-1]
    sums = block_sums(alive, vectors)
    last, sums = lax.optimization_barrier((rows[-1], sums))
    last = lax.ppermute(last, "grp", there[-1])
    mine = pack(meta, sums, heads)
    mine, *rows = lax.optimization_barrier((mine, *rows[:-1]))
    rows = [lax.ppermute(x, "grp", pairs) for x, pairs in zip(rows, there)]
    order = sorted(range(chips - 1), key=lambda i: (i + 1 == chips - 1, i == 0))
    near = [lax.ppermute(mine, "row", along[i]) for i in order]
    sums, totals = with_prior(blocks, [mine] + near, old_centroids)
    near, last = lax.optimization_barrier((near, last))
    both = jnp.concatenate([mine] + near, axis=0)
    rows.append(last)
    far = lax.ppermute(both, "row", cores)
    table, norms, share, part = make_table(n_rows, blocks, far, sums, totals, rows[-1])
    parts = [*parts_of(norms, table, rows[:-1]), part]
    parts = [lax.ppermute(x, "grp", pairs) for x, pairs in zip(parts, back)]
    scores = scores_of(alive, norms, table, vectors)
    scores = merge(picks, alive, parts, scores)
    return (share, scores)


def solution(mesh):
    in_specs = (
        P(("grp", "row"), None),
        P(("grp", "row")),
        P(("grp", "row")),
        P(),
        P(),
        P("grp", None),
    )
    out_specs = (P(("grp", "row"), None), P(("grp", "row"), None))
    return jax.shard_map(local, mesh=mesh, in_specs=in_specs, out_specs=out_specs, check_vma=False)
```

```python
import functools
import math

import jax
import jax.numpy as jnp
from jax import lax
from jax.experimental import pallas as pl
from jax.experimental.pallas import tpu as pltpu
from jax.sharding import PartitionSpec as P

PRIOR = 16
TAIL = 4
MIB = 1 << 20
F32 = jnp.float32
BF16 = jnp.bfloat16
I16 = jnp.int16
I32 = jnp.int32
ROW_DIMS = (((1,), (1,)), ((), ()))
COL_DIMS = (((0,), (0,)), ((), ()))
VMEM = pl.BlockSpec(memory_space=pltpu.VMEM)
SMEM = pl.BlockSpec(memory_space=pltpu.SMEM)
HBM = pl.BlockSpec(memory_space=pltpu.HBM)


def peer(index, step, size):
    if size & (size - 1) == 0:
        return index ^ step
    return (index + step) % size


def power(exponent):
    return jnp.exp2(exponent).astype(BF16).astype(F32)


def iota(shape, dim):
    return lax.broadcasted_iota(I32, shape, dim)


def shaped(shape, dtype):
    return jax.ShapeDtypeStruct(shape, dtype)


def params(mib):
    return pltpu.CompilerParams(vmem_limit_bytes=mib * MIB)


def cost(flops, size):
    return pl.CostEstimate(flops=flops, bytes_accessed=size, transcendentals=0)


def in_hbm(array):
    return pltpu.with_memory_space_constraint(array, pltpu.HBM)


def as_lanes(column):
    rows = column.shape[0]
    wide = jnp.broadcast_to(column, (rows, 128))
    return jnp.transpose(jnp.concatenate([wide, jnp.zeros((128 - rows, 128), F32)], axis=0))[0:1, :]


def coded_rows(values):
    largest = jnp.maximum(jnp.max(jnp.abs(values), axis=1, keepdims=True), 2.0**-80)
    exponent = jnp.ceil(jnp.log2(largest) + 0.001) - 15.0
    return jnp.round(values * power(-exponent)).astype(I32), exponent


def turned_weights(weights):
    return jnp.transpose(jnp.broadcast_to(weights, (128, 128)))


def movers_kernel(n_groups, lists_group, list_ref, pos_ref, counts_ref, keep_ref, vec_ref, *refs):
    steps = n_groups - 1
    alive_ref, meta_ref, picks_ref = refs[:3]
    head_refs, row_refs = refs[3 : 3 + steps], refs[3 + steps : 3 + 2 * steps]
    lists, pos, fill, held, sems = refs[3 + 2 * steps :]
    loads = [
        pltpu.make_async_copy(src, dst, sems.at[steps + i])
        for i, (src, dst) in enumerate([(list_ref, lists), (pos_ref, pos), (counts_ref, fill), (keep_ref, held)])
    ]
    for load in loads:
        load.start()
    blocks, block = keep_ref.shape
    group = lax.axis_index("grp")
    base = (group * lax.axis_size("row") + lax.axis_index("row")) * blocks
    shift = lists_group.bit_length() - 1
    lane = iota((1, block), 1)
    row = iota((blocks, block), 0)
    slots = jnp.full((1, block), -1, I32)
    filled = jnp.zeros((blocks, block), I32)
    picks = [jnp.int32(-1)] * steps
    homes = [jnp.int32(-1)] * steps
    for load in loads[:2]:
        load.wait()
    for b in range(blocks):
        home = pos[lists[base + b]]
        home_group = home >> shift if lists_group == 1 << shift else home // lists_group
        slot = home - home_group * lists_group
        slots = jnp.where((lane == b) & (home_group == group), slot, slots)
        for k in range(steps):
            hit = home_group == peer(group, k + 1, n_groups)
            picks[k] = jnp.where(hit, b, picks[k])
            homes[k] = jnp.where(hit, slot, homes[k])
    fetches = []
    for k in range(steps):
        picks_ref[k] = picks[k]
        start = pl.multiple_of(jnp.maximum(picks[k], 0) * block, block)
        fetches.append(pltpu.make_async_copy(vec_ref.at[pl.ds(start, block), :], row_refs[k], sems.at[k]))
        fetches[k].start()
    for load in loads[2:]:
        load.wait()
    for b in range(blocks):
        filled = jnp.where(row == b, fill[b], filled)
    alive = held[...].astype(F32) * (iota((blocks, block), 1) < filled).astype(F32)
    alive_ref[...] = alive
    ones = jnp.ones((8, block), BF16)
    block_counts = lax.dot_general(ones, alive.astype(BF16), ROW_DIMS, preferred_element_type=F32)
    meta_ref[...] = jnp.zeros_like(meta_ref)
    meta_ref[0:1, :] = slots.astype(F32)
    meta_ref[1:2, 0:blocks] = block_counts[0:1, :]
    for k in range(steps):
        fetches[k].wait()
        weights = alive_ref[pl.ds(jnp.maximum(picks[k], 0), 1), :]
        wide = jnp.broadcast_to(weights, (16, block)).astype(BF16)
        total = jnp.dot(wide, row_refs[k][...], preferred_element_type=F32)
        chunks = total.shape[1] // 128
        for j in range(chunks):
            head_refs[k][j : j + 1, :] = total[0:1, j * 128 : (j + 1) * 128]
        head_refs[k][chunks : chunks + 8, :] = jnp.concatenate(
            [
                jnp.broadcast_to(jnp.sum(weights, axis=1, keepdims=True), (1, 128)),
                jnp.broadcast_to(homes[k].astype(F32), (1, 128)),
                jnp.zeros((6, 128), F32),
            ],
            axis=0,
        )


def movers(n_groups, lists_group, block_list, home_pos, counts, keep, vectors):
    steps = n_groups - 1
    blocks, block = keep.shape
    width = vectors.shape[1]
    outs = pl.pallas_call(
        functools.partial(movers_kernel, n_groups, lists_group),
        out_shape=[shaped((blocks, block), F32), shaped((8, block), F32), shaped((steps,), I32)]
        + [shaped((width // 128 + 8, 128), F32)] * steps
        + [shaped((block, width), BF16)] * steps,
        in_specs=[HBM] * 5,
        out_specs=[VMEM, VMEM, SMEM] + [VMEM] * (2 * steps),
        scratch_shapes=[
            pltpu.SMEM(block_list.shape, I32),
            pltpu.SMEM(home_pos.shape, I32),
            pltpu.SMEM(counts.shape, I32),
            pltpu.VMEM(keep.shape, I32),
            pltpu.SemaphoreType.DMA((steps + 4,)),
        ],
        compiler_params=params(8),
        cost_estimate=cost(2 * steps * block * width, 6 * steps * block * width),
        name="movers",
    )(*map(in_hbm, (block_list, home_pos, counts, keep, vectors)))
    return outs[0], outs[1], outs[2], outs[3 : 3 + steps], outs[3 + steps :]


def sums_kernel(alive_ref, vec_ref, sums_ref):
    blocks, block = alive_ref.shape
    tile = 8
    row = iota((tile, block), 0)
    for t in range(blocks // tile):
        alive = alive_ref[t * tile : (t + 1) * tile, :]
        spread = jnp.concatenate([jnp.where(row == j, alive, 0.0) for j in range(tile)], axis=1)
        rows = vec_ref[t * tile * block : (t + 1) * tile * block, :]
        sums_ref[t * tile : (t + 1) * tile, :] = jnp.dot(spread.astype(BF16), rows, preferred_element_type=F32)


def block_sums(alive, vectors):
    blocks = alive.shape[0]
    rows, width = vectors.shape
    return pl.pallas_call(
        sums_kernel,
        out_shape=shaped((blocks, width), F32),
        in_specs=[VMEM] * 2,
        out_specs=VMEM,
        compiler_params=params(16),
        cost_estimate=cost(16 * rows * width, 2 * rows * width),
        name="block_sums",
    )(alive, vectors)


def pack_kernel(meta_ref, sums_ref, *refs):
    heads, out_ref = refs[:-1][::-1], refs[-1]
    blocks, width = sums_ref.shape
    chunks = width // 128
    lane = iota((1, 128), 1)
    slots, counts = meta_ref[0:1, :], meta_ref[1:2, :]
    arrived = []
    for k, head in enumerate(heads):
        arrived.append(jnp.concatenate([head[j : j + 1, :] for j in range(chunks)], axis=1))
        slots = jnp.where(lane == blocks + k, head[chunks + 1 : chunks + 2, :], slots)
        counts = jnp.where(lane == blocks + k, head[chunks : chunks + 1, :], counts)
    coded, exponent = coded_rows(jnp.concatenate([sums_ref[...]] + arrived, axis=0))
    facts = jnp.concatenate([slots, counts, as_lanes(exponent)], axis=1).astype(I32)
    facts = jnp.concatenate([facts, jnp.zeros((1, width - 384), I32)], axis=1)
    tail = jnp.concatenate([coded[blocks:]] + [jnp.zeros((1, width), I32)] * (TAIL - 1 - len(heads)) + [facts], axis=0)
    parts = [coded[j : j + 8] for j in range(0, blocks, 8)]
    parts.append(jnp.concatenate([tail[:, : width // 2], tail[:, width // 2 :]], axis=0))
    out_ref[...] = jnp.concatenate(parts, axis=1).astype(I16)


def pack(meta, sums, heads):
    blocks, width = sums.shape
    size = blocks // 8 * width + width // 2
    return pl.pallas_call(
        pack_kernel,
        out_shape=shaped((8, size), I16),
        in_specs=[VMEM] * (2 + len(heads)),
        out_specs=VMEM,
        compiler_params=params(8),
        cost_estimate=cost(6 * 10**9, 48 * size),
        name="pack",
    )(meta, sums, *heads[::-1])


def unpacked(packed, blocks, width):
    big = jnp.concatenate([packed[:, j * width : (j + 1) * width] for j in range(blocks // 8)], axis=0)
    tail = packed[:, blocks // 8 * width :]
    return big, jnp.concatenate([tail[:TAIL], tail[TAIL:]], axis=1)


def add_up(sources, blocks, lists, width):
    sources = [unpacked(x, blocks, width) for x in sources]
    fill = len(sources) % 2
    big = jnp.concatenate([x for x, _ in sources], axis=0)
    small = jnp.concatenate([x for _, x in sources] + [jnp.zeros((TAIL, width), I32)] * fill, axis=0)

    def lanes(which, spare):
        facts = [x[TAIL - 1 :, 128 * which : 128 * which + 128].astype(F32) for _, x in sources]
        wide = jnp.concatenate([x[:, 0:blocks] for x in facts], axis=1)
        tail = [x[:, blocks : blocks + TAIL] for x in facts] + [jnp.full((1, TAIL), spare, F32)] * fill
        return wide, jnp.concatenate(tail, axis=1)

    def four(pair, low=True):
        wide, tail = pair
        return jnp.concatenate([wide, wide * low, tail, tail * low], axis=1)

    slots = four(lanes(0, -1.0))
    counts = four(lanes(1, 0.0), low=False)
    scale, scale_small = map(power, lanes(2, 0.0))
    scale = jnp.concatenate([256.0 * scale, scale, 256.0 * scale_small, scale_small], axis=1)
    hit = iota((lists, slots.shape[1]), 0) == slots.astype(I32)
    totals = jnp.sum(jnp.where(hit, counts, 0.0), axis=1, keepdims=True)
    values = jnp.concatenate([big >> 8, big & 255, small >> 8, small & 255], axis=0)
    sums = jnp.dot(
        jnp.where(hit, scale, 0.0).astype(BF16), values.astype(F32).astype(BF16), preferred_element_type=F32
    )
    return sums, totals


def prior_kernel(blocks, *refs):
    near, (old_ref, sums_ref, totals_ref) = refs[:-3], refs[-3:]
    lists = old_ref.shape[0]
    prior = 1.0 * PRIOR
    sums, totals = add_up([ref[...].astype(I32) for ref in near], blocks, lists, old_ref.shape[1])
    sums_ref[...] = sums + prior * old_ref[...].astype(F32)
    totals_ref[...] = jnp.broadcast_to(totals + prior, totals_ref.shape)


def with_prior(blocks, near, old):
    lists, width = old.shape
    return pl.pallas_call(
        functools.partial(prior_kernel, blocks),
        out_shape=[shaped((lists, width), F32), shaped((lists, 128), F32)],
        in_specs=[VMEM] * (1 + len(near)),
        out_specs=[VMEM] * 2,
        compiler_params=params(16),
        cost_estimate=cost(20000 * lists * width, 8 * lists * width),
        name="prior",
    )(*near, old)


def table_kernel(blocks, far, sums_ref, totals_ref, row_ref, table_ref, norms_ref, share_ref, part_ref):
    lists, width = sums_ref.shape
    far_all = far[...].astype(I32)
    sources = [far_all[j : j + 8] for j in range(0, far.shape[0], 8)]
    sums, totals = add_up(sources, blocks, lists, width)
    totals = totals_ref[:, 0:1] + totals
    table = ((sums_ref[...] + sums) * (1.0 / totals)).astype(BF16)
    table_ref[...] = table
    share = share_ref.shape[0]
    start = pl.multiple_of(lax.axis_index("row") * share, share)
    share_ref[...] = table_ref[pl.ds(start, share), :]
    squares = jnp.square(table.astype(F32))
    partial = squares[:, 0:128]
    for j in range(1, width // 128):
        partial = partial + squares[:, j * 128 : (j + 1) * 128]
    ones = jnp.ones((16, 128), BF16)
    norms = jnp.zeros((16, lists), F32)
    for _ in range(3):
        piece = partial.astype(BF16)
        partial = partial - piece.astype(F32)
        norms = norms + lax.dot_general(ones, piece, ROW_DIMS, preferred_element_type=F32)
    factor = 1.0 / math.sqrt(width)
    norms = norms * factor
    norms_ref[...] = norms[0:8]
    dots = lax.dot_general(row_ref[...], table, ROW_DIMS, preferred_element_type=F32)
    part_ref[...] = (dots * (2.0 * factor) - norms[0:1, :]).astype(part_ref.dtype)


def make_table(n_rows, blocks, far, sums, totals, rows):
    lists, width = sums.shape
    return pl.pallas_call(
        functools.partial(table_kernel, blocks),
        out_shape=[
            shaped((lists, width), BF16),
            shaped((8, lists), F32),
            shaped((lists // n_rows, width), BF16),
            shaped((rows.shape[0], lists), BF16),
        ],
        in_specs=[VMEM] * 4,
        out_specs=[VMEM] * 4,
        compiler_params=params(24),
        cost_estimate=cost(2000 * lists * width, 8 * lists * width),
        name="table",
    )(far, sums, totals, rows)


def parts_kernel(norms_ref, table_ref, *refs):
    steps = len(refs) // 2
    factor = 1.0 / math.sqrt(table_ref.shape[1])
    norms = norms_ref[0:1, :]
    for row_ref, part_ref in zip(refs[:steps], refs[steps:]):
        dots = lax.dot_general(row_ref[...], table_ref[...], ROW_DIMS, preferred_element_type=F32)
        part_ref[...] = (dots * (2.0 * factor) - norms).astype(part_ref.dtype)


def parts_of(norms, table, rows):
    lists, width = table.shape
    block = rows[0].shape[0]
    return pl.pallas_call(
        parts_kernel,
        out_shape=[shaped((block, lists), BF16)] * len(rows),
        in_specs=[VMEM] * (2 + len(rows)),
        out_specs=[VMEM] * len(rows),
        compiler_params=params(16),
        cost_estimate=cost(2 * len(rows) * block * lists * width, 2 * lists * width),
        name="parts",
    )(norms, table, *rows)


def scores_kernel(alive_ref, norms_ref, table_ref, vec_ref, out_ref, held, sems):
    blocks, block = alive_ref.shape
    lists, width = table_ref.shape
    factor = 1.0 / math.sqrt(width)
    norms = norms_ref[0:1, :]
    table = table_ref[...]
    tile = 2
    stores = []
    for t in range(blocks // tile):
        span = slice(t * tile * block, (t + 1) * tile * block)
        dots = lax.dot_general(vec_ref[span, :], table, ROW_DIMS, preferred_element_type=F32)
        for j in range(tile):
            b = t * tile + j
            weights = jnp.concatenate([turned_weights(alive_ref[b : b + 1, :])] * (lists // 128), axis=1)
            part = dots[j * block : (j + 1) * block, :]
            held[b * block : (b + 1) * block, :] = (part * (2.0 * factor) - norms) * weights
        stores.append(pltpu.make_async_copy(held.at[span, :], out_ref.at[span, :], sems.at[t]))
        stores[t].start()
    for store in stores:
        store.wait()


def scores_of(alive, norms, table, vectors):
    blocks = alive.shape[0]
    rows, width = vectors.shape
    lists = table.shape[0]
    return pl.pallas_call(
        scores_kernel,
        out_shape=shaped((rows, lists), F32),
        in_specs=[VMEM] * 4,
        out_specs=HBM,
        scratch_shapes=[pltpu.VMEM((rows, lists), F32), pltpu.SemaphoreType.DMA((blocks // 2,))],
        compiler_params=params(24),
        cost_estimate=cost(2 * lists * rows * width, 4 * rows * lists),
        name="scores",
    )(alive, norms, table, vectors)


def merge_kernel(picks_ref, alive_ref, *refs):
    steps = picks_ref.shape[0]
    parts, out_ref, held, sems = refs[:steps], refs[steps + 1], refs[steps + 2], refs[steps + 3]
    block, lists = parts[0].shape

    half = block // 2

    def store(k, part):
        start = pl.multiple_of(picks_ref[k] * block + part * half, half)
        here = held.at[k, pl.ds(part * half, half), :]
        return pltpu.make_async_copy(here, out_ref.at[pl.ds(start, half), :], sems.at[2 * k + part])

    for k in range(steps):

        @pl.when(picks_ref[k] >= 0)
        def _():
            weights = turned_weights(alive_ref[pl.ds(picks_ref[k], 1), :])
            weights = jnp.concatenate([weights] * (lists // 128), axis=1)
            for part in range(2):
                at = slice(part * half, (part + 1) * half)
                held[k, at, :] = parts[k][at, :].astype(F32) * weights[at, :]
                store(k, part).start()

    for k in range(steps):

        @pl.when(picks_ref[k] >= 0)
        def _():
            store(k, 0).wait()
            store(k, 1).wait()


def merge(picks, alive, parts, scores):
    steps = len(parts)
    block, lists = parts[0].shape
    return pl.pallas_call(
        merge_kernel,
        out_shape=shaped(scores.shape, scores.dtype),
        in_specs=[SMEM, VMEM] + [VMEM] * steps + [HBM],
        out_specs=HBM,
        scratch_shapes=[pltpu.VMEM((steps, block, lists), F32), pltpu.SemaphoreType.DMA((2 * steps,))],
        input_output_aliases={2 + steps: 0},
        compiler_params=params(8),
        cost_estimate=cost(2 * steps * block * lists, 6 * steps * block * lists),
        name="merge",
    )(picks, alive, *parts, scores)


def local(vectors, keep_bits, counts, block_list, home_pos, old_centroids):
    n_groups = lax.axis_size("grp")
    n_rows = lax.axis_size("row")
    blocks = counts.shape[0]
    block = vectors.shape[0] // blocks
    lists_group = old_centroids.shape[0]
    keep = keep_bits.reshape(blocks, block)
    there = [[(i, peer(i, k, n_groups)) for i in range(n_groups)] for k in range(1, n_groups)]
    back = [[(j, i) for i, j in pairs] for pairs in there]
    chips = n_rows // 2
    along = [[(i, 2 * peer(i // 2, k, chips) + i % 2) for i in range(n_rows)] for k in range(1, chips)]
    cores = [(i, i ^ 1) for i in range(n_rows)]

    alive, meta, picks, heads, rows = movers(n_groups, lists_group, block_list, home_pos, counts, keep, vectors)
    heads = [lax.ppermute(x, "grp", pairs) for x, pairs in zip(heads[::-1], there[::-1])][::-1]
    sums = block_sums(alive, vectors)
    last, sums = lax.optimization_barrier((rows[-1], sums))
    last = lax.ppermute(last, "grp", there[-1])
    mine = pack(meta, sums, heads)
    mine, *rows = lax.optimization_barrier((mine, *rows[:-1]))
    rows = [lax.ppermute(x, "grp", pairs) for x, pairs in zip(rows, there)]
    order = sorted(range(chips - 1), key=lambda i: (i + 1 == chips - 1, i == 0))
    near = [lax.ppermute(mine, "row", along[i]) for i in order]
    sums, totals = with_prior(blocks, [mine] + near, old_centroids)
    near, last = lax.optimization_barrier((near, last))
    both = jnp.concatenate([mine] + near, axis=0)
    rows.append(last)
    far = lax.ppermute(both, "row", cores)
    table, norms, share, part = make_table(n_rows, blocks, far, sums, totals, rows[-1])
    parts = [*parts_of(norms, table, rows[:-1]), part]
    parts = [lax.ppermute(x, "grp", pairs) for x, pairs in zip(parts, back)]
    scores = scores_of(alive, norms, table, vectors)
    scores = merge(picks, alive, parts, scores)
    return (share, scores)


def solution(mesh):
    in_specs = (
        P(("grp", "row"), None),
        P(("grp", "row")),
        P(("grp", "row")),
        P(),
        P(),
        P("grp", None),
    )
    out_specs = (P(("grp", "row"), None), P(("grp", "row"), None))
    return jax.shard_map(local, mesh=mesh, in_specs=in_specs, out_specs=out_specs, check_vma=False)
```
